256 devices in a mesh: pt: 16 (over y, x_lo, core), anc: 2 (over x_hi), head: 8 (over z).
Axes of the slice: x: 4 (x_hi: 2, x_lo: 2; x = x_hi * 2 + x_lo), y: 4, z: 8, core: 2. Of those that a mesh axis runs over, the one named last changes fastest.
Arguments:
- points: bfloat16 [8192, 1024], P(('pt', 'anc'), 'head'), may hold values from -6 to 6
- anchor_index: int32 [8192], replicated, may hold values from 0 to 8191
- tile_branch: int32 [32], P(('pt', 'anc')), may hold values 0 or 1
- norm_gain: float32 [1024], replicated, may hold values from 0.5 to 2
- q_surface: bfloat16 [1024, 1024], P(None, 'head'), as said below
- q_volume: bfloat16 [1024, 1024], P(None, 'head'), as said below
- kv_weight: bfloat16 [2, 1024, 1024], P(None, None, 'head'), may hold values from -0.1875 to 0.1875
- out_weight: bfloat16 [1024, 1024], P('head'), may hold values from -1.5 to 1.5
Outputs:
- point_update: bfloat16 [8192, 1024], P(('pt', 'anc'), 'head')
- anchor_update: bfloat16 [8192, 1024], P(('pt', 'anc'), 'head')
The draws below stay inside these ranges and needn't reach their ends.
Inputs may be any that keep to these rules, and one draw needn't show every extreme that they name: `anchor_index`: every anchor names one query point; two anchors may name the same one. `q_surface`: entries of mean zero. `q_volume`: entries of mean zero.
All inputs are finite; a program needn't handle non-finite values. No bound on the sum of `tile_branch` on one device may be relied on, other than what follows from the above.
Results may differ from the reference program's by a relative error of at most 0.02.
The reference program's roundings to bfloat16 on the way count: a program that leaves them out, or rounds other values in their place, can miss the bound.
Values may be sent and summed in bfloat16 or wider, within the bound.
A program may use at most 64 MiB of HBM per device.

```python
import math
import jax
import jax.numpy as jnp
from jax import lax

D = 1024
HEADS = 16
HEAD_DIM = 64
TILE = 256
NPTS = 8192
NANC = 8192
NTILES = 32


def query_weight(key):
    return (jax.random.normal(key, (D, D), jnp.float32) * D ** (-0.5)).astype(jnp.bfloat16)


def draw_q_surface(key, part):
    key = jax.random.fold_in(key, 11)
    return query_weight(key)


def draw_q_volume(key, part):
    key = jax.random.fold_in(key, 23)
    return query_weight(key)


def with_ends(drawn, key, low, largest):
    longest = drawn.shape.index(max(drawn.shape))
    spots = []
    for shift in (0, 1):
        where = [jax.random.randint(jax.random.fold_in(key, axis), (), 0, length) for axis, length in enumerate(drawn.shape)]
        where[longest] = (where[longest] + shift) % drawn.shape[longest]
        spots.append(tuple(where))
    return drawn.at[spots[0]].set(low).at[spots[1]].set(largest)


def shard_levels(key, extent, cuts, smallest, top_value):
    def one(axis_at, parts):
        heights = jax.random.uniform(jax.random.fold_in(jax.random.fold_in(key, 6), axis_at), (parts,), jnp.float32, smallest / len(cuts), top_value / len(cuts))
        return jnp.repeat(jnp.exp(heights), extent[axis_at] // parts).reshape((-1,) + (1,) * (len(extent) - axis_at - 1))

    gain = one(*cuts[0])
    for cut in cuts[1:]:
        gain = gain * one(*cut)
    return gain


def scatter_about(own_key, extent, deviation, limit, cuts=(), kind=jnp.bfloat16):
    loudness = shard_levels(own_key, extent, cuts, -0.22, 0.18) if cuts else 1.0
    result = jax.random.normal(own_key, extent, jnp.float32) * deviation * loudness
    return jnp.minimum(jnp.maximum(result, -limit), limit).astype(kind)


def setup_inputs(seed: int = 0) -> dict:
    arg_keys = jax.random.split(jax.random.key(seed), 9)
    points = scatter_about(arg_keys[0], (NPTS, D), 1.0, 6.0, ((0, 32), (1, 8)))
    anchor_index = with_ends(jax.random.randint(arg_keys[1], (NANC,), 0, NPTS), jax.random.fold_in(arg_keys[1], 1), 0, NPTS - 1).astype(jnp.int32)
    tile_branch = with_ends((jax.random.randint(arg_keys[2], (NTILES,), 0, 3) < 1).astype(jnp.int32), jax.random.fold_in(arg_keys[2], 1), 0, 1)
    norm_gain = jnp.clip(jnp.exp(jax.random.uniform(arg_keys[3], (D,), jnp.float32, math.log(0.5), math.log(2.0))), 0.5, 2.0)
    q_surface = draw_q_surface(jax.random.fold_in(arg_keys[8], 71), 0)
    q_volume = draw_q_volume(jax.random.fold_in(arg_keys[8], 71), 0)
    kv_weight = scatter_about(arg_keys[6], (2, D, D), D ** -0.5, 0.1875, ((2, 8),))
    out_weight = scatter_about(arg_keys[7], (D, D), 16 ** -0.5, 1.5, ((0, 8),))
    return {"points": points, "anchor_index": anchor_index, "tile_branch": tile_branch, "norm_gain": norm_gain, "q_surface": q_surface, "q_volume": q_volume, "kv_weight": kv_weight, "out_weight": out_weight}


def attend(queries, flags, keys, values):
    half = keys.shape[0] // 2
    volume_key = jnp.arange(keys.shape[0]) >= half
    key_heads = keys.astype(jnp.float32).reshape(keys.shape[0], HEADS, HEAD_DIM)
    value_heads = values.astype(jnp.float32).reshape(values.shape[0], HEADS, HEAD_DIM)
    blocks = queries.reshape(queries.shape[0] // TILE, TILE, HEADS, HEAD_DIM)

    def one_block(item):
        query_block, open_all = item
        scores = jnp.einsum('qhd,khd->hqk', query_block.astype(jnp.float32), key_heads) / jnp.sqrt(jnp.float32(HEAD_DIM))
        visible = jnp.logical_or(open_all == 1, volume_key)[None, None, :]
        scores = jnp.where(visible, scores, jnp.float32(-1e+30))
        peak = lax.optimization_barrier(jnp.max(scores, axis=-1, keepdims=True))
        weights = jnp.where(visible, jnp.exp(scores - peak), jnp.float32(0.0))
        totals = lax.optimization_barrier(jnp.sum(weights, axis=-1))
        rounded = weights.astype(jnp.bfloat16).astype(jnp.float32)
        mixed = jnp.einsum('hqk,khd->qhd', rounded, value_heads) / jnp.transpose(totals)[:, :, None]
        return mixed.reshape(TILE, HEADS * HEAD_DIM).astype(jnp.bfloat16)
    out = lax.map(one_block, (blocks, flags))
    return out.reshape(queries.shape[0], HEADS * HEAD_DIM)

def reference(points, anchor_index, tile_branch, norm_gain, q_surface, q_volume, kv_weight, out_weight):
    values_in = points.astype(jnp.float32)
    scale = lax.rsqrt(lax.optimization_barrier(jnp.mean(values_in * values_in, axis=-1, keepdims=True)) + 1e-06)
    normed = (values_in * scale * norm_gain[None, :]).astype(jnp.bfloat16)
    anchors = jnp.take(normed, anchor_index, axis=0)
    keys = jnp.dot(anchors, kv_weight[0], preferred_element_type=jnp.float32).astype(jnp.bfloat16)
    values = jnp.dot(anchors, kv_weight[1], preferred_element_type=jnp.float32).astype(jnp.bfloat16)
    row_surface = jnp.repeat(tile_branch, TILE) == 1
    point_queries = jnp.where(row_surface[:, None], jnp.dot(normed, q_surface, preferred_element_type=jnp.float32), jnp.dot(normed, q_volume, preferred_element_type=jnp.float32)).astype(jnp.bfloat16)
    half = anchors.shape[0] // 2
    anchor_surface = jnp.arange(anchors.shape[0]) < half
    anchor_queries = jnp.where(anchor_surface[:, None], jnp.dot(anchors, q_surface, preferred_element_type=jnp.float32), jnp.dot(anchors, q_volume, preferred_element_type=jnp.float32)).astype(jnp.bfloat16)
    point_mixed = attend(point_queries, tile_branch, keys, values)
    anchor_flags = jnp.ones((anchors.shape[0] // TILE,), jnp.int32)
    anchor_mixed = attend(anchor_queries, anchor_flags, keys, values)
    point_update = jnp.dot(point_mixed, out_weight, preferred_element_type=jnp.float32).astype(jnp.bfloat16)
    anchor_update = jnp.dot(anchor_mixed, out_weight, preferred_element_type=jnp.float32).astype(jnp.bfloat16)
    return (point_update, anchor_update)
```

```python
import functools

import jax
import jax.numpy as jnp
from jax import lax
from jax.experimental import pallas as pl
from jax.experimental.pallas import tpu as pltpu
from jax.sharding import PartitionSpec as P

MESH = pl.DeviceIdType.MESH
F32 = jnp.float32
BF16 = jnp.bfloat16
NEG = -1e30
T = 256
W = 128
G = 32
NZ = 8
NX = 4
LANES = 128


def group_of(x, y, c):
    return y * 8 + lax.rem(x, 2) * 4 + c * 2 + x // 2


def device_of(x, y, c, z):
    return (y * 4 + lax.rem(x, 2) * 2 + c, x // 2, z)


def nt(a, b):
    return lax.dot_general(a, b, (((1,), (1,)), ((), ())), preferred_element_type=F32)


def dot(a, b):
    return jnp.dot(a, b, preferred_element_type=F32)


class Copies:
    def __init__(self, send, recv):
        self.send, self.recv, self.count, self.sent = send, recv, 0, []

    def new(self):
        self.count += 1
        return self.count - 1

    def start(self, k, src, dst, device):
        copy = pltpu.make_async_remote_copy(
            src_ref=src,
            dst_ref=dst,
            send_sem=self.send.at[k],
            recv_sem=self.recv.at[k],
            device_id=device,
            device_id_type=MESH,
        )
        copy.start()
        self.sent.append(copy)

    def wait(self, k, landed):
        pltpu.make_async_remote_copy(
            src_ref=landed,
            dst_ref=landed,
            send_sem=self.send.at[k],
            recv_sem=self.recv.at[k],
            device_id=self.home,
            device_id_type=MESH,
        ).wait_recv()

    def drain(self):
        for copy in self.sent:
            copy.wait_send()
        self.sent = []


N_COPIES = 120


def kernel(
    points, idx, branch, gain, wqs, wqv, wkv, wo,
    outp, outa,
    gp, nrm, vqs, vqv, vkv, vwo, wcols, kv, qsv, qa, qx, qstage, qz, bias, stat, acc, mixed, mg,
    wsem, send, recv,
):
    pt, anc, z = lax.axis_index("pt"), lax.axis_index("anc"), lax.axis_index("head")
    c = lax.rem(pt, 2)
    x = anc * 2 + lax.rem(pt // 2, 2)
    y = pt // 4
    me = group_of(x, y, c)
    cp = Copies(send, recv)
    cp.home = (pt, anc, z)

    def step(i, d, n):
        return lax.rem(i + d + n, n)

    peers = [device_of(x, y, c, step(z, d, NZ)) for d in range(1, NZ)]
    peers += [device_of(step(x, d, NX), y, c, z) for d in range(1, NX)]
    peers += [device_of(x, step(y, d, NX), c, z) for d in range(1, NX)]
    sibling = device_of(x, y, 1 - c, z)
    peers += [sibling]
    barrier = pltpu.get_barrier_semaphore()
    for peer in peers:
        pl.semaphore_signal(barrier, inc=1, device_id=peer, device_id_type=MESH)

    weights = [
        pltpu.make_async_copy(src, dst, wsem.at[i])
        for i, (src, dst) in enumerate(((wqs, vqs), (wqv, vqv), (wkv, vkv), (wo, vwo)))
    ]
    for copy in weights:
        copy.start()
    gp[z] = points[...]
    pl.semaphore_wait(barrier, len(peers))

    def z_up(d):
        return device_of(x, y, c, step(z, d, NZ))

    def z_gather(own, buf):
        ids = [cp.new() for _ in range(8)]
        low, high = pl.ds(0, T // 2), pl.ds(T // 2, T // 2)

        def begin():
            cp.start(ids[0], own, buf.at[z], z_up(1))
            cp.start(ids[1], own, buf.at[z], z_up(-1))

        def hop(n):
            left, right = step(z, -n, NZ), step(z, n, NZ)

            def run():
                cp.wait(ids[2 * n - 2], buf.at[left])
                if n < 3:
                    cp.start(ids[2 * n], buf.at[left], buf.at[left], z_up(1))
                else:
                    cp.start(ids[6], buf.at[left, low], buf.at[left, low], z_up(1))
                cp.wait(ids[2 * n - 1], buf.at[right])
                if n < 3:
                    cp.start(ids[2 * n + 1], buf.at[right], buf.at[right], z_up(-1))
                else:
                    cp.start(ids[7], buf.at[right, high], buf.at[right, high], z_up(-1))

            return run

        def end():
            far = step(z, 4, NZ)
            cp.wait(ids[6], buf.at[far, low])
            cp.wait(ids[7], buf.at[far, high])

        return [begin, hop(1), hop(2), hop(3), end]

    gather = z_gather(points, gp)
    gather[0]()

    def tally(first, count):
        total = jnp.zeros((64, LANES), F32)
        for i in range(count):
            row = idx[:, pl.ds((first + i) * 1024, 1024)]
            high = (row // 128 == lax.broadcasted_iota(jnp.int32, (64, 1024), 0)).astype(F32)
            low = (lax.rem(row, 128) == lax.broadcasted_iota(jnp.int32, (128, 1024), 0)).astype(F32)
            total = total + nt(high.astype(BF16), low.astype(BF16))
        return total

    surface = tally(0, 4)
    gather[1]()
    volume = tally(4, 4)
    gather[2]()
    everyone = surface + volume

    def log_count(n):
        return jnp.where(n > 0.0, jnp.log(jnp.maximum(n, 1.0)), NEG)

    open_all = branch[0] == 1
    bias[0] = log_count(jnp.where(open_all, everyone, volume))
    bias[1] = log_count(everyone)
    gather[3]()
    for copy in weights:
        copy.wait()
    gather[4]()

    total = jnp.zeros((T, LANES), F32)
    for i in range(NZ):
        part = gp[i].astype(F32)
        total = total + part * part
    scale = lax.rsqrt(jnp.sum(total, axis=-1, keepdims=True) * (1.0 / 1024.0) + 1e-06)
    for i in range(NZ):
        columns = pl.ds(i * W, W)
        nrm[:, columns] = (gp[i].astype(F32) * scale * gain[:, columns]).astype(BF16)
    qsv[0] = dot(nrm[...], vqs[...]).astype(BF16) * BF16(0.125)
    qsv[1] = dot(nrm[...], vqv[...]).astype(BF16) * BF16(0.125)

    mine = y // 2
    qa[c, y] = qsv[mine]
    q_ids = [cp.new() for _ in range(3)]
    for d in (1, 2, 3):
        there = step(y, d, NX)
        cp.start(q_ids[d - 1], qsv.at[there // 2], qa.at[c, y], device_of(x, there, c, z))

    kv[me, :, 0:W] = dot(nrm[...], vkv[0]).astype(BF16)
    kv[me, :, W : 2 * W] = dot(nrm[...], vkv[1]).astype(BF16)

    u, v = (1 - c) * x + c * y, (1 - c) * y + c * x

    def place(i, j):
        return (1 - c) * i + c * j, (1 - c) * j + c * i

    def block(du, dv):
        bx, by = place(step(u, du, NX), step(v, dv, NX))
        return group_of(bx, by, c)

    def sibling_block(du, dv):
        bx, by = place(step(u, dv, NX), step(v, du, NX))
        return group_of(bx, by, 1 - c)

    def toward(du, dv):
        bx, by = place(step(u, du, NX), step(v, dv, NX))
        return device_of(bx, by, c, z)

    low, high = pl.ds(0, T // 2), pl.ds(T // 2, T // 2)
    u_ids = [cp.new() for _ in range(4)]
    v_ids = [[cp.new() for _ in range(4)] for _ in range(4)]
    s_ids = [[cp.new() for _ in range(4)] for _ in range(4)]

    def share(du):
        g = block(du, 0)
        cp.start(v_ids[du][0], kv.at[g], kv.at[g], toward(0, 1))
        cp.start(v_ids[du][1], kv.at[g], kv.at[g], toward(0, -1))

    def across(du, dv):
        g = block(du, dv)
        cp.start(s_ids[du][dv], kv.at[g], kv.at[g], sibling)

    def from_sibling(du, dv):
        cp.wait(s_ids[du][dv], kv.at[sibling_block(du, dv)])

    def begin_kv():
        g = block(0, 0)
        cp.start(u_ids[0], kv.at[g], kv.at[g], toward(1, 0))
        cp.start(u_ids[1], kv.at[g], kv.at[g], toward(-1, 0))
        share(0)
        across(0, 0)

    def u_hop():
        g = block(3, 0)
        cp.wait(u_ids[0], kv.at[g])
        cp.start(u_ids[2], kv.at[g, low], kv.at[g, low], toward(1, 0))
        g = block(1, 0)
        cp.wait(u_ids[1], kv.at[g])
        cp.start(u_ids[3], kv.at[g, high], kv.at[g, high], toward(-1, 0))
        for du in (3, 1):
            share(du)
            across(du, 0)

    def u_end():
        g = block(2, 0)
        cp.wait(u_ids[2], kv.at[g, low])
        cp.wait(u_ids[3], kv.at[g, high])
        share(2)
        across(2, 0)

    def v_hop(du):
        g = block(du, 3)
        cp.wait(v_ids[du][0], kv.at[g])
        cp.start(v_ids[du][2], kv.at[g, low], kv.at[g, low], toward(0, 1))
        across(du, 3)
        g = block(du, 1)
        cp.wait(v_ids[du][1], kv.at[g])
        cp.start(v_ids[du][3], kv.at[g, high], kv.at[g, high], toward(0, -1))
        across(du, 1)

    def v_end(du):
        g = block(du, 2)
        cp.wait(v_ids[du][2], kv.at[g, low])
        cp.wait(v_ids[du][3], kv.at[g, high])
        across(du, 2)

    begin_kv()
    w_ids = [cp.new() for _ in range(7)]
    for d in range(1, NZ):
        to = step(z, d, NZ)
        cp.start(w_ids[d - 1], vwo.at[:, pl.ds(pl.multiple_of(to * W, W), W)], wcols.at[z], z_up(d))
    wcols[z] = vwo[:, pl.ds(pl.multiple_of(z * W, W), W)]

    u_hop()

    for d in (1, 2, 3):
        cp.wait(q_ids[d - 1], qa.at[c, step(y, -d, NX)])
    q_sib = cp.new()
    cp.start(q_sib, qa.at[c], qa.at[c], sibling)
    u_end()
    v_hop(0)
    cp.wait(q_sib, qa.at[1 - c])

    x_ids = [cp.new() for _ in range(3)]
    for d in (1, 2, 3, 0):
        there = step(x, d, NX)
        g = group_of(there, y, c)
        for half in range(2):
            named = idx[:, pl.ds(pl.multiple_of(g * T + half * LANES, LANES), LANES)]
            named = jnp.transpose(jnp.broadcast_to(named, (LANES, LANES)))
            named = jnp.concatenate([named, named], axis=1)
            found = jnp.zeros((LANES, W), F32)
            for core in range(2):
                for row in range(NX):
                    base = group_of(x, row, core) * T
                    here = named - base == lax.broadcasted_iota(jnp.int32, (LANES, T), 1)
                    found = found + dot(here.astype(F32).astype(BF16), qa[core, row])
            rows = pl.ds(half * LANES, LANES)
            if d:
                qstage[d - 1, rows] = found.astype(BF16)
            else:
                qx[x, rows] = found.astype(BF16)
        if d:
            cp.start(x_ids[d - 1], qstage.at[d - 1], qx.at[x], device_of(there, y, c, z))
    v_end(0)
    for du in (3, 1, 2):
        v_hop(du)
        v_end(du)
    for du in range(4):
        for dv in range(4):
            from_sibling(du, dv)
    for d in (1, 2, 3):
        cp.wait(x_ids[d - 1], qx.at[step(x, -d, NX)])

    lane = lax.broadcasted_iota(jnp.int32, (T, W), 1)

    def split_heads(t, rows):
        rows = rows.astype(F32)
        qz[t, 0] = jnp.where(lane < 64, rows, 0.0).astype(BF16)
        qz[t, 1] = jnp.where(lane < 64, 0.0, rows).astype(BF16)

    split_heads(0, jnp.where(open_all, qsv[0].astype(F32), qsv[1].astype(F32)))
    split_heads(1, sum(qx[i].astype(F32) for i in range(NX)))

    stat[...] = jnp.full(stat.shape, 2.0 * NEG, F32)
    acc[...] = jnp.zeros(acc.shape, F32)
    ones = jnp.ones((T, LANES), BF16)

    def absorb(t, h, blocks):
        scores = []
        for g in blocks:
            s = nt(qz[t, h], kv[g, :, 0:W])
            extra = jnp.concatenate([bias[t, pl.ds(2 * g, 1)], bias[t, pl.ds(2 * g + 1, 1)]], axis=1)
            scores.append(s + extra)
        top = functools.reduce(jnp.maximum, scores)
        top = jnp.max(top, axis=-1, keepdims=True)
        old = stat[t, h]
        new = jnp.maximum(old, jnp.broadcast_to(top, (T, LANES)))
        factor = jnp.exp(old - new)
        stat[t, h] = new
        wide = jnp.concatenate([new, new], axis=1)
        added = None
        for g, s in zip(blocks, scores):
            p = jnp.exp(s - wide).astype(BF16)
            term = dot(p, jnp.concatenate([kv[g, :, W : 2 * W], ones], axis=1))
            added = term if added is None else added + term
        acc[t, h] = acc[t, h] * jnp.concatenate([factor, factor], axis=1) + added

    def finish(t):
        parts = [acc[t, h, :, 0:W] / acc[t, h, :, W : 2 * W] for h in range(2)]
        mixed[t] = jnp.where(lane < 64, parts[0], parts[1]).astype(BF16)
        mg[t, z] = mixed[t]

    def project(t, out):
        rows = jnp.concatenate([mg[t, i] for i in range(NZ)], axis=1)
        out[...] = dot(rows, wcols[...].reshape(NZ * W, W)).astype(BF16)

    for t in range(2):
        def one(i, carry):
            for h in range(2):
                absorb(t, h, [2 * i, 2 * i + 1])
            return carry

        lax.fori_loop(0, G // 2, one, 0)
        finish(t)

    gathers = [z_gather(mixed.at[t], mg.at[t]) for t in range(2)]
    for parts in zip(*gathers):
        for part in parts:
            part()
    for d in range(1, NZ):
        cp.wait(w_ids[d - 1], wcols.at[step(z, -d, NZ)])
    project(0, outp)
    project(1, outa)
    cp.drain()


def shards(points, anchor_index, tile_branch, norm_gain, q_surface, q_volume, kv_weight, out_weight):
    vmem = pl.BlockSpec(memory_space=pltpu.VMEM)
    anywhere = pl.BlockSpec(memory_space=pl.ANY)
    smem = pl.BlockSpec(memory_space=pltpu.SMEM)
    return pl.pallas_call(
        kernel,
        out_shape=(
            jax.ShapeDtypeStruct((T, W), BF16),
            jax.ShapeDtypeStruct((T, W), BF16),
        ),
        in_specs=[vmem, vmem, smem, vmem, anywhere, anywhere, anywhere, anywhere],
        out_specs=(vmem, vmem),
        scratch_shapes=[
            pltpu.VMEM((NZ, T, W), BF16),
            pltpu.VMEM((T, NZ * W), BF16),
            pltpu.VMEM((NZ * W, W), BF16),
            pltpu.VMEM((NZ * W, W), BF16),
            pltpu.VMEM((2, NZ * W, W), BF16),
            pltpu.VMEM((W, NZ * W), BF16),
            pltpu.VMEM((NZ, W, W), BF16),
            pltpu.VMEM((G, T, 2 * W), BF16),
            pltpu.VMEM((2, T, W), BF16),
            pltpu.VMEM((2, NX, T, W), BF16),
            pltpu.VMEM((NX, T, W), BF16),
            pltpu.VMEM((3, T, W), BF16),
            pltpu.VMEM((2, 2, T, W), BF16),
            pltpu.VMEM((2, 64, LANES), F32),
            pltpu.VMEM((2, 2, T, LANES), F32),
            pltpu.VMEM((2, 2, T, 2 * W), F32),
            pltpu.VMEM((2, T, W), BF16),
            pltpu.VMEM((2, NZ, T, W), BF16),
            pltpu.SemaphoreType.DMA((4,)),
            pltpu.SemaphoreType.DMA((N_COPIES,)),
            pltpu.SemaphoreType.DMA((N_COPIES,)),
        ],
        compiler_params=pltpu.CompilerParams(
            collective_id=0, has_side_effects=True, vmem_limit_bytes=50 * 1024 * 1024
        ),
    )(
        points,
        anchor_index.reshape(1, -1),
        tile_branch,
        norm_gain.reshape(1, -1),
        q_surface,
        q_volume,
        kv_weight,
        out_weight,
    )


def solution(mesh):
    in_specs = (
        P(("pt", "anc"), "head"),
        P(),
        P(("pt", "anc")),
        P(),
        P(None, "head"),
        P(None, "head"),
        P(None, None, "head"),
        P("head", None),
    )
    out_specs = (P(("pt", "anc"), "head"), P(("pt", "anc"), "head"))
    return jax.shard_map(shards, mesh=mesh, in_specs=in_specs, out_specs=out_specs, check_vma=False)
```

```python
import jax
import jax.numpy as jnp
from jax import lax
from jax.experimental import pallas as pl
from jax.experimental.pallas import tpu as pltpu
from jax.sharding import PartitionSpec as P

MESH = pl.DeviceIdType.MESH
F32 = jnp.float32
BF16 = jnp.bfloat16
NEG = -1e30
T = 256
W = 128
G = 32
NZ = 8
NX = 4
LANES = 128
D = 1024
N_COPIES = 128
CHUNK = 4
ORDER = (
    (0, 0), (3, 0), (1, 0), (0, 3),
    (0, 1), (2, 0), (3, 3), (3, 1),
    (1, 3), (1, 1), (0, 2), (2, 3),
    (2, 1), (3, 2), (1, 2), (2, 2),
)
SLOT = {pair: i for i, pair in enumerate(ORDER)}


def group_of(x, y, c):
    return y * 8 + lax.rem(x, 2) * 4 + c * 2 + x // 2


def device_of(x, y, c, z):
    return (y * 4 + lax.rem(x, 2) * 2 + c, x // 2, z)


def nt(a, b):
    return lax.dot_general(a, b, (((1,), (1,)), ((), ())), preferred_element_type=F32)


def dot(a, b):
    return jnp.dot(a, b, preferred_element_type=F32)


class Copies:
    def __init__(self, send, recv, home):
        self.send, self.recv, self.home, self.count, self.sent = send, recv, home, 0, []

    def new(self):
        self.count += 1
        return self.count - 1

    def make(self, k, src, dst, device):
        return pltpu.make_async_remote_copy(
            src_ref=src,
            dst_ref=dst,
            send_sem=self.send.at[k],
            recv_sem=self.recv.at[k],
            device_id=device,
            device_id_type=MESH,
        )

    def start(self, k, src, dst, device):
        copy = self.make(k, src, dst, device)
        copy.start()
        self.sent.append(copy)

    def wait(self, k, landed):
        self.make(k, landed, landed, self.home).wait_recv()

    def drain(self):
        for copy in self.sent:
            copy.wait_send()


def kernel(
    points, idx_in, branch, gain_in, wqs, wqv, wkv, wo,
    outp, outa,
    idx, gain, gp, nrm, vqs, vqv, vkv, vwo, wcols, kv, ext, logs, qsv, qa, qx, qstage, qe,
    stat, acc, even, odd, mg,
    wsem, send, recv,
):
    pt, anc, z = lax.axis_index("pt"), lax.axis_index("anc"), lax.axis_index("head")
    c = lax.rem(pt, 2)
    x = anc * 2 + lax.rem(pt // 2, 2)
    y = pt // 4
    cp = Copies(send, recv, (pt, anc, z))

    def step(i, d, n):
        return lax.rem(i + d + n, n)

    peers = [device_of(x, y, c, step(z, d, NZ)) for d in range(1, NZ)]
    peers += [device_of(step(x, d, NX), y, c, z) for d in range(1, NX)]
    peers += [device_of(x, step(y, d, NX), c, z) for d in range(1, NX)]
    sibling = device_of(x, y, 1 - c, z)
    peers += [sibling]
    barrier = pltpu.get_barrier_semaphore()
    for peer in peers:
        pl.semaphore_signal(barrier, inc=1, device_id=peer, device_id_type=MESH)

    pairs = (
        (points, gp.at[z]), (idx_in, idx), (gain_in, gain),
        (wkv, vkv), (wqs, vqs), (wqv, vqv), (wo, vwo),
    )
    loads = [pltpu.make_async_copy(src, dst, wsem.at[i]) for i, (src, dst) in enumerate(pairs)]
    for load in loads:
        load.start()
    loads[0].wait()
    pl.semaphore_wait(barrier, len(peers))

    def z_up(d):
        return device_of(x, y, c, step(z, d, NZ))

    low, high = pl.ds(0, T // 2), pl.ds(T // 2, T // 2)

    def z_gather(buf):
        ids = [cp.new() for _ in range(8)]

        def begin():
            for k, d in enumerate((2, -2, 1, -1)):
                cp.start(ids[k], buf.at[z], buf.at[z], z_up(d))

        def forward():
            at = step(z, -2, NZ)
            cp.wait(ids[0], buf.at[at])
            cp.start(ids[4], buf.at[at], buf.at[at], z_up(1))
            cp.start(ids[6], buf.at[at, low], buf.at[at, low], z_up(2))
            at = step(z, 2, NZ)
            cp.wait(ids[1], buf.at[at])
            cp.start(ids[5], buf.at[at], buf.at[at], z_up(-1))
            cp.start(ids[7], buf.at[at, high], buf.at[at, high], z_up(-2))

        def end():
            for k, d in ((2, -1), (3, 1), (4, -3), (5, 3)):
                cp.wait(ids[k], buf.at[step(z, d, NZ)])
            at = step(z, 4, NZ)
            cp.wait(ids[6], buf.at[at, low])
            cp.wait(ids[7], buf.at[at, high])

        return begin, forward, end

    begin, forward, end = z_gather(gp)
    begin()

    def tally(first, count):
        total = jnp.zeros((64, LANES), F32)
        for i in range(count):
            row = idx[:, pl.ds((first + i) * 1024, 1024)]
            upper = (row // 128 == lax.broadcasted_iota(jnp.int32, (64, 1024), 0)).astype(F32)
            lower = (lax.rem(row, 128) == lax.broadcasted_iota(jnp.int32, (128, 1024), 0)).astype(F32)
            total = total + nt(upper.astype(BF16), lower.astype(BF16))
        return total

    loads[1].wait()
    surface = tally(0, 4)
    volume = tally(4, 4)
    everyone = surface + volume
    open_all = branch[0] == 1

    def log_count(n):
        return jnp.where(n > 0.0, jnp.log(jnp.maximum(n, 1.0)), NEG)

    for t, n in enumerate((jnp.where(open_all, everyone, volume), everyone)):
        rest = log_count(n)
        for j in range(3):
            term = rest.astype(BF16).astype(F32)
            logs[3 * t + j] = term
            rest = rest - term
    forward()

    u, v = (1 - c) * x + c * y, (1 - c) * y + c * x

    def place(i, j):
        return (1 - c) * i + c * j, (1 - c) * j + c * i

    def group_at(slot):
        du, dv = ORDER[slot % 16]
        if slot < 16:
            bx, by = place(step(u, du, NX), step(v, dv, NX))
            return group_of(bx, by, c)
        bx, by = place(step(u, dv, NX), step(v, du, NX))
        return group_of(bx, by, 1 - c)

    sub = lax.broadcasted_iota(jnp.int32, (8, LANES), 0)
    for slot in range(G):
        g = group_at(slot)
        for half in range(2):
            terms = jnp.zeros((8, LANES), F32)
            for j in range(6):
                terms = jnp.where(sub == j, logs[j, pl.ds(2 * g + half, 1)], terms)
            terms = jnp.concatenate([terms, jnp.zeros((LANES - 8, LANES), F32)], axis=0)
            ext[slot, pl.ds(half * LANES, LANES)] = jnp.transpose(terms).astype(BF16)

    for load in loads[2:]:
        load.wait()
    end()

    total = jnp.zeros((T, LANES), F32)
    for i in range(NZ):
        part = gp[i].astype(F32)
        total = total + part * part
    scale = lax.rsqrt(jnp.sum(total, axis=-1, keepdims=True) * (1.0 / D) + 1e-06)
    for i in range(NZ):
        columns = pl.ds(i * W, W)
        nrm[:, columns] = (gp[i].astype(F32) * scale * gain[:, columns]).astype(BF16)
    keys = dot(nrm[...], vkv[0]).astype(BF16)
    kv[0, W : 2 * W, 0:LANES] = keys[:LANES]
    kv[0, W : 2 * W, LANES : 2 * LANES] = keys[LANES:]
    kv[0, 0:W] = jnp.transpose(dot(nrm[...], vkv[1])).astype(BF16)
    qsv[0] = dot(nrm[...], vqs[...]).astype(BF16) * BF16(0.125)
    qsv[1] = dot(nrm[...], vqv[...]).astype(BF16) * BF16(0.125)

    def toward(du, dv):
        bx, by = place(step(u, du, NX), step(v, dv, NX))
        return device_of(bx, by, c, z)

    u_ids = [cp.new() for _ in range(4)]
    v_ids = [[cp.new() for _ in range(4)] for _ in range(4)]
    s_ids = [cp.new() for _ in range(16)]

    def pass_on(k, src, dst, device, rows=None):
        src, dst = SLOT[src], SLOT[dst]
        if rows is None:
            cp.start(k, kv.at[src], kv.at[dst], device)
        else:
            cp.start(k, kv.at[src, rows], kv.at[dst, rows], device)

    def landed(k, pair, rows=None):
        slot = SLOT[pair]
        cp.wait(k, kv.at[slot] if rows is None else kv.at[slot, rows])

    def share(du):
        pass_on(v_ids[du][0], (du, 0), (du, 3), toward(0, 1))
        pass_on(v_ids[du][1], (du, 0), (du, 1), toward(0, -1))

    def across(pair):
        slot = SLOT[pair]
        cp.start(s_ids[slot], kv.at[slot], kv.at[16 + slot], sibling)

    def from_sibling(first, count):
        for slot in range(first, first + count):
            cp.wait(s_ids[slot], kv.at[16 + slot])

    def u_hop():
        landed(u_ids[0], (3, 0))
        pass_on(u_ids[2], (3, 0), (2, 0), toward(1, 0), low)
        share(3)
        landed(u_ids[1], (1, 0))
        pass_on(u_ids[3], (1, 0), (2, 0), toward(-1, 0), high)
        share(1)
        across((3, 0))
        across((1, 0))

    def u_end():
        landed(u_ids[2], (2, 0), low)
        landed(u_ids[3], (2, 0), high)
        share(2)
        across((2, 0))

    def v_hop(du):
        landed(v_ids[du][0], (du, 3))
        pass_on(v_ids[du][2], (du, 3), (du, 2), toward(0, 1), low)
        landed(v_ids[du][1], (du, 1))
        pass_on(v_ids[du][3], (du, 1), (du, 2), toward(0, -1), high)
        across((du, 3))
        across((du, 1))

    def v_end(du):
        landed(v_ids[du][2], (du, 2), low)
        landed(v_ids[du][3], (du, 2), high)
        across((du, 2))

    pass_on(u_ids[0], (0, 0), (3, 0), toward(1, 0))
    pass_on(u_ids[1], (0, 0), (1, 0), toward(-1, 0))
    share(0)

    mine = y // 2
    q_ids = [cp.new() for _ in range(4)]
    for d in (1, 2, 3):
        there = step(y, d, NX)
        cp.start(q_ids[d], qsv.at[there // 2], qa.at[c, y], device_of(x, there, c, z))
    qa[c, y] = qsv[mine]
    across((0, 0))

    w_ids = [cp.new() for _ in range(NZ)]
    for d in range(1, NZ):
        to = pl.multiple_of(step(z, d, NZ) * W, W)
        cp.start(w_ids[d], vwo.at[:, pl.ds(to, W)], wcols.at[z], z_up(d))
    wcols[z] = vwo[:, pl.ds(pl.multiple_of(z * W, W), W)]

    lane = lax.broadcasted_iota(jnp.int32, (T, W), 1)

    def split_heads(t, rows):
        marks = jnp.where(lane // 3 == t, 1.0, 0.0).astype(BF16)
        for h in range(2):
            qe[t, h, :, 0:W] = jnp.where(lane // 64 == h, rows, 0.0).astype(BF16)
            qe[t, h, :, W : 2 * W] = marks

    split_heads(0, jnp.where(open_all, qsv[0].astype(F32), qsv[1].astype(F32)))
    stat[...] = jnp.full(stat.shape, 2.0 * NEG, F32)
    acc[...] = jnp.zeros(acc.shape, F32)
    ones = jnp.ones((16, T), BF16)

    def fill(t, h, first, buf):
        top = None
        for j in range(CHUNK):
            slot = first + j
            k = jnp.concatenate([kv[slot, W : 2 * W, 0:LANES], kv[slot, W : 2 * W, LANES : 2 * LANES]], axis=0)
            s = nt(jnp.concatenate([k, ext[slot]], axis=1), qe[t, h])
            buf[j] = s
            top = s if top is None else jnp.maximum(top, s)
        return jnp.max(top, axis=0, keepdims=True)

    def absorb(t, h, first, buf, top):
        old = stat[t, h, 0:1]
        new = jnp.maximum(old, top)
        factor = jnp.exp(old - new)
        stat[t, h, 0:1] = new
        added = None
        for j in range(CHUNK):
            p = jnp.exp(buf[j] - new).astype(BF16)
            values = jnp.concatenate([kv[first + j, pl.ds(h * 64, 64)], ones], axis=0)
            term = dot(values, p)
            added = term if added is None else added + term
        acc[t, h] = acc[t, h] * factor + added

    def attend(t, first, chunks):
        last = first + (chunks - 1) * CHUNK
        top = fill(t, 0, first, even)

        def one(i, top):
            at = first + i * CHUNK
            other = fill(t, 1, at, odd)
            absorb(t, 0, at, even, top)
            top = fill(t, 0, jnp.minimum(at + CHUNK, last), even)
            absorb(t, 1, at, odd, other)
            return top

        if chunks > 1:
            top = lax.fori_loop(0, chunks - 1, one, top)
        other = fill(t, 1, last, odd)
        absorb(t, 0, last, even, top)
        absorb(t, 1, last, odd, other)

    def finish(t):
        parts = [acc[t, h, 0:64] / acc[t, h, 64:65] for h in range(2)]
        mg[t, z] = jnp.transpose(jnp.concatenate(parts, axis=0)).astype(BF16)

    def project(t, out):
        rows = jnp.concatenate([mg[t, i] for i in range(NZ)], axis=1)
        out[...] = dot(rows, wcols[...].reshape(NZ * W, W)).astype(BF16)

    x_ids = [cp.new() for _ in range(4)]

    def select():
        for d in (1, 2, 3, 0):
            there = step(x, d, NX)
            g = group_of(there, y, c)
            for half in range(2):
                named = idx[:, pl.ds(pl.multiple_of(g * T + half * LANES, LANES), LANES)]
                named = jnp.transpose(jnp.broadcast_to(named, (LANES, LANES)))
                named = jnp.concatenate([named, named], axis=1)
                found = jnp.zeros((LANES, W), F32)
                for core in range(2):
                    for row in range(NX):
                        base = group_of(x, row, core) * T
                        here = named - base == lax.broadcasted_iota(jnp.int32, (LANES, T), 1)
                        found = found + dot(here.astype(F32).astype(BF16), qa[core, row])
                rows = pl.ds(half * LANES, LANES)
                if d:
                    qstage[d - 1, rows] = found.astype(BF16)
                else:
                    qx[x, rows] = found.astype(BF16)
            if d:
                cp.start(x_ids[d], qstage.at[d - 1], qx.at[x], device_of(there, y, c, z))

    u_hop()
    for d in (1, 2, 3):
        cp.wait(q_ids[d], qa.at[c, step(y, -d, NX)])
    cp.start(q_ids[0], qa.at[c], qa.at[c], sibling)
    v_hop(0)
    attend(0, 0, 1)
    u_end()
    v_hop(3)
    v_hop(1)
    cp.wait(q_ids[0], qa.at[1 - c])
    select()
    v_end(0)
    v_hop(2)
    attend(0, 4, 2)
    v_end(3)
    v_end(1)
    from_sibling(0, 8)
    attend(0, 16, 2)
    v_end(2)
    attend(0, 12, 1)
    for d in (1, 2, 3):
        cp.wait(x_ids[d], qx.at[step(x, -d, NX)])
    split_heads(1, sum(qx[i].astype(F32) for i in range(NX)))
    attend(1, 0, 6)
    from_sibling(8, 8)
    attend(0, 24, 2)
    finish(0)
    point_steps = z_gather(mg.at[0])
    point_steps[0]()
    attend(1, 24, 2)
    point_steps[1]()
    finish(1)
    anchor_steps = z_gather(mg.at[1])
    anchor_steps[0]()
    for d in range(1, NZ):
        cp.wait(w_ids[d], wcols.at[step(z, -d, NZ)])
    point_steps[2]()
    anchor_steps[1]()
    project(0, outp)
    anchor_steps[2]()
    project(1, outa)
    cp.drain()


def shards(points, anchor_index, tile_branch, norm_gain, q_surface, q_volume, kv_weight, out_weight):
    vmem = pl.BlockSpec(memory_space=pltpu.VMEM)
    anywhere = pl.BlockSpec(memory_space=pl.ANY)
    smem = pl.BlockSpec(memory_space=pltpu.SMEM)
    return pl.pallas_call(
        kernel,
        out_shape=(
            jax.ShapeDtypeStruct((T, W), BF16),
            jax.ShapeDtypeStruct((T, W), BF16),
        ),
        in_specs=[anywhere, anywhere, smem, anywhere, anywhere, anywhere, anywhere, anywhere],
        out_specs=(vmem, vmem),
        scratch_shapes=[
            pltpu.VMEM((1, G * T), jnp.int32),
            pltpu.VMEM((1, D), F32),
            pltpu.VMEM((NZ, T, W), BF16),
            pltpu.VMEM((T, D), BF16),
            pltpu.VMEM((D, W), BF16),
            pltpu.VMEM((D, W), BF16),
            pltpu.VMEM((2, D, W), BF16),
            pltpu.VMEM((W, D), BF16),
            pltpu.VMEM((NZ, W, W), BF16),
            pltpu.VMEM((G, 2 * W, T), BF16),
            pltpu.VMEM((G, T, LANES), BF16),
            pltpu.VMEM((8, 64, LANES), F32),
            pltpu.VMEM((2, T, W), BF16),
            pltpu.VMEM((2, NX, T, W), BF16),
            pltpu.VMEM((NX, T, W), BF16),
            pltpu.VMEM((3, T, W), BF16),
            pltpu.VMEM((2, 2, T, 2 * W), BF16),
            pltpu.VMEM((2, 2, 8, T), F32),
            pltpu.VMEM((2, 2, 80, T), F32),
            pltpu.VMEM((CHUNK, T, T), F32),
            pltpu.VMEM((CHUNK, T, T), F32),
            pltpu.VMEM((2, NZ, T, W), BF16),
            pltpu.SemaphoreType.DMA((7,)),
            pltpu.SemaphoreType.DMA((N_COPIES,)),
            pltpu.SemaphoreType.DMA((N_COPIES,)),
        ],
        compiler_params=pltpu.CompilerParams(
            collective_id=0, has_side_effects=True, vmem_limit_bytes=60 * 1024 * 1024
        ),
    )(
        points,
        anchor_index.reshape(1, -1),
        tile_branch,
        norm_gain.reshape(1, -1),
        q_surface,
        q_volume,
        kv_weight,
        out_weight,
    )


def solution(mesh):
    in_specs = (
        P(("pt", "anc"), "head"),
        P(),
        P(("pt", "anc")),
        P(),
        P(None, "head"),
        P(None, "head"),
        P(None, None, "head"),
        P("head", None),
    )
    out_specs = (P(("pt", "anc"), "head"), P(("pt", "anc"), "head"))
    return jax.shard_map(shards, mesh=mesh, in_specs=in_specs, out_specs=out_specs, check_vma=False)
```

```python
import jax
import jax.numpy as jnp
from jax import lax
from jax.experimental import pallas as pl
from jax.experimental.pallas import tpu as pltpu
from jax.sharding import PartitionSpec as P

MESH = pl.DeviceIdType.MESH
F32 = jnp.float32
BF16 = jnp.bfloat16
NEG = -1e30
T = 256
W = 128
G = 32
NZ = 8
NX = 4
LANES = 128
D = 1024
N_COPIES = 128
H = T // 2
PART = T // NZ
CHUNK = 4
ORDER = (
    (0, 0), (3, 0), (1, 0), (2, 0),
    (0, 3), (0, 1), (3, 3), (3, 1),
    (1, 3), (1, 1), (2, 3), (2, 1),
    (0, 2), (3, 2), (1, 2), (2, 2),
)
SLOT = {pair: i for i, pair in enumerate(ORDER)}


def group_of(x, y, c):
    return y * 8 + lax.rem(x, 2) * 4 + c * 2 + x // 2


def device_of(x, y, c, z):
    return (y * 4 + lax.rem(x, 2) * 2 + c, x // 2, z)


def nt(a, b):
    return lax.dot_general(a, b, (((1,), (1,)), ((), ())), preferred_element_type=F32)


def dot(a, b):
    return jnp.dot(a, b, preferred_element_type=F32)


class Copies:
    def __init__(self, send, recv, home):
        self.send, self.recv, self.home, self.count, self.sent = send, recv, home, 0, []

    def new(self):
        self.count += 1
        return self.count - 1

    def make(self, k, src, dst, device):
        return pltpu.make_async_remote_copy(
            src_ref=src,
            dst_ref=dst,
            send_sem=self.send.at[k],
            recv_sem=self.recv.at[k],
            device_id=device,
            device_id_type=MESH,
        )

    def start(self, k, src, dst, device):
        copy = self.make(k, src, dst, device)
        copy.start()
        self.sent.append(copy)

    def wait(self, k, landed):
        self.make(k, landed, landed, self.home).wait_recv()

    def drain(self, count):
        for copy in self.sent[:count]:
            copy.wait_send()
        self.sent = self.sent[count:]


def kernel(
    points, idx_in, branch, gain_in, wqs, wqv, wkv, wo,
    out,
    idx, gain, gp, nrm, vqs, vqv, vkv, wall, kv, ext, logs, qsv, qa, qx, qstage, qe,
    stat, acc, even, odd, mixed, rows_in, rows_out, done,
    wsem, send, recv,
):
    pt, anc, z = lax.axis_index("pt"), lax.axis_index("anc"), lax.axis_index("head")
    c = lax.rem(pt, 2)
    x = anc * 2 + lax.rem(pt // 2, 2)
    y = pt // 4
    cp = Copies(send, recv, (pt, anc, z))

    def step(i, d, n):
        return lax.rem(i + d + n, n)

    peers = [device_of(x, y, c, step(z, d, NZ)) for d in range(1, NZ)]
    peers += [device_of(step(x, d, NX), y, c, z) for d in range(1, NX)]
    peers += [device_of(x, step(y, d, NX), c, z) for d in range(1, NX)]
    sibling = device_of(x, y, 1 - c, z)
    peers += [sibling]
    barrier = pltpu.get_barrier_semaphore()
    for peer in peers:
        pl.semaphore_signal(barrier, inc=1, device_id=peer, device_id_type=MESH)

    pairs = (
        (points.at[pl.ds(0, H)], gp.at[0, z]), (points.at[pl.ds(H, H)], gp.at[1, z]), (idx_in, idx), (gain_in, gain),
        (wkv, vkv), (wqs, vqs), (wqv, vqv),
        (wo.at[pl.ds(0, W // 2)], wall.at[z, 0]), (wo.at[pl.ds(W // 2, W // 2)], wall.at[z, 1]),
    )
    loads = [pltpu.make_async_copy(src, dst, wsem.at[i]) for i, (src, dst) in enumerate(pairs)]
    for load in loads:
        load.start()
    loads[0].wait()
    loads[1].wait()
    pl.semaphore_wait(barrier, len(peers))

    def z_up(d):
        return device_of(x, y, c, step(z, d, NZ))


    def z_gather(at, rows):
        ids = [cp.new() for _ in range(8)]
        first, second = pl.ds(0, rows // 2), pl.ds(rows // 2, rows // 2)

        def begin():
            for k, d in enumerate((2, -2, 1, -1)):
                cp.start(ids[k], at(z), at(z), z_up(d))

        def forward():
            here = at(step(z, -2, NZ))
            cp.wait(ids[0], here)
            cp.start(ids[4], here, here, z_up(1))
            cp.start(ids[6], here.at[first], here.at[first], z_up(2))
            here = at(step(z, 2, NZ))
            cp.wait(ids[1], here)
            cp.start(ids[5], here, here, z_up(-1))
            cp.start(ids[7], here.at[second], here.at[second], z_up(-2))

        def near():
            cp.wait(ids[2], at(step(z, -1, NZ)))
            cp.wait(ids[3], at(step(z, 1, NZ)))

        def end():
            cp.wait(ids[4], at(step(z, -3, NZ)))
            cp.wait(ids[5], at(step(z, 3, NZ)))
            here = at(step(z, 4, NZ))
            cp.wait(ids[6], here.at[first])
            cp.wait(ids[7], here.at[second])

        return begin, forward, near, end

    halves = [z_gather(lambda i, e=e: gp.at[e, i], H) for e in range(2)]
    for begin, _, _, _ in halves:
        begin()

    def tally(first, count):
        total = jnp.zeros((64, LANES), F32)
        for i in range(count):
            row = idx[:, pl.ds((first + i) * 1024, 1024)]
            upper = (row // 128 == lax.broadcasted_iota(jnp.int32, (64, 1024), 0)).astype(F32)
            lower = (lax.rem(row, 128) == lax.broadcasted_iota(jnp.int32, (128, 1024), 0)).astype(F32)
            total = total + nt(upper.astype(BF16), lower.astype(BF16))
        return total

    loads[2].wait()
    surface = tally(0, 4)
    volume = tally(4, 4)
    everyone = surface + volume
    open_all = branch[0] == 1

    def log_count(n):
        return jnp.where(n > 0.0, jnp.log(jnp.maximum(n, 1.0)), NEG)

    for t, n in enumerate((jnp.where(open_all, everyone, volume), everyone)):
        rest = log_count(n)
        for j in range(3):
            term = rest.astype(BF16).astype(F32)
            logs[3 * t + j] = term
            rest = rest - term
    for _, forward, _, _ in halves:
        forward()

    u, v = (1 - c) * x + c * y, (1 - c) * y + c * x

    def place(i, j):
        return (1 - c) * i + c * j, (1 - c) * j + c * i

    def group_at(slot):
        du, dv = ORDER[slot % 16]
        if slot < 16:
            bx, by = place(step(u, du, NX), step(v, dv, NX))
            return group_of(bx, by, c)
        bx, by = place(step(u, dv, NX), step(v, du, NX))
        return group_of(bx, by, 1 - c)

    sub = lax.broadcasted_iota(jnp.int32, (8, LANES), 0)
    for slot in range(G):
        g = group_at(slot)
        for half in range(2):
            terms = jnp.zeros((8, LANES), F32)
            for j in range(6):
                terms = jnp.where(sub == j, logs[j, pl.ds(2 * g + half, 1)], terms)
            terms = jnp.concatenate([terms, jnp.zeros((LANES - 8, LANES), F32)], axis=0)
            ext[slot, pl.ds(half * LANES, LANES)] = jnp.transpose(terms).astype(BF16)

    for load in loads[3:]:
        load.wait()

    def project_half(e):
        total = jnp.zeros((H, LANES), F32)
        for i in range(NZ):
            part = gp[e, i].astype(F32)
            total = total + part * part
        scale = lax.rsqrt(jnp.sum(total, axis=-1, keepdims=True) * (1.0 / D) + 1e-06)
        for i in range(NZ):
            columns = pl.ds(i * W, W)
            nrm[e, :, columns] = (gp[e, i].astype(F32) * scale * gain[:, columns]).astype(BF16)
        kv[0, e, W : 2 * W] = dot(nrm[e], vkv[0]).astype(BF16)
        kv[0, e, 0:W] = jnp.transpose(dot(nrm[e], vkv[1])).astype(BF16)

    def toward(du, dv):
        bx, by = place(step(u, du, NX), step(v, dv, NX))
        return device_of(bx, by, c, z)

    u_ids = [[cp.new() for _ in range(3)] for _ in range(2)]
    v_ids = [[[cp.new() for _ in range(3)] for _ in range(4)] for _ in range(2)]
    s_ids = [cp.new() for _ in range(16)]

    def pass_on(k, e, src, dst, device):
        cp.start(k, kv.at[SLOT[src], e], kv.at[SLOT[dst], e], device)

    def landed(k, e, pair):
        cp.wait(k, kv.at[SLOT[pair], e])

    def share(e, du):
        pass_on(v_ids[e][du][0], e, (du, 0), (du, 3), toward(0, 1))
        pass_on(v_ids[e][du][1], e, (du, 0), (du, 1), toward(0, -1))

    def across(*pairs):
        for pair in pairs:
            slot = SLOT[pair]
            cp.start(s_ids[slot], kv.at[slot], kv.at[16 + slot], sibling)

    def from_sibling(first, count):
        for slot in range(first, first + count):
            cp.wait(s_ids[slot], kv.at[16 + slot])

    def kv_begin(e):
        pass_on(u_ids[e][0], e, (0, 0), (3, 0), toward(1, 0))
        pass_on(u_ids[e][1], e, (0, 0), (1, 0), toward(-1, 0))
        share(e, 0)
        pass_on(u_ids[e][2], e, (0, 0), (2, 0), toward(2, 0))

    def u_hop(e):
        for k, du in ((0, 3), (1, 1), (2, 2)):
            landed(u_ids[e][k], e, (du, 0))
            share(e, du)

    def v_hop(e, du):
        landed(v_ids[e][du][e], e, (du, 3 - 2 * e))
        pass_on(v_ids[e][du][2], e, (du, 3 - 2 * e), (du, 2), toward(0, 1 - 2 * e))

    def v_rest(du):
        landed(v_ids[1][du][0], 1, (du, 3))
        landed(v_ids[0][du][1], 0, (du, 1))
        across((du, 3), (du, 1))

    def v_end(du):
        landed(v_ids[0][du][2], 0, (du, 2))
        landed(v_ids[1][du][2], 1, (du, 2))
        across((du, 2))

    halves[0][2]()
    halves[0][3]()
    project_half(0)
    kv_begin(0)
    halves[1][2]()
    halves[1][3]()
    w_begin, w_forward, w_near, w_end = z_gather(lambda i: wall.at[i, c], W // 2)
    w_ids = [cp.new() for _ in range(NZ)]

    def w_across(*distances):
        for d in distances:
            at = step(z, d, NZ)
            cp.start(w_ids[d], wall.at[at, c], wall.at[at, c], sibling)

    def w_wait():
        for d in range(1, NZ):
            cp.wait(w_ids[d], wall.at[step(z, d, NZ), 1 - c])

    w_begin()
    project_half(1)
    kv_begin(1)
    rows = nrm[...].reshape(T, D)
    qsv[0] = dot(rows, vqs[...]).astype(BF16) * BF16(0.125)
    qsv[1] = dot(rows, vqv[...]).astype(BF16) * BF16(0.125)

    mine = y // 2
    q_ids = [cp.new() for _ in range(4)]
    for d in (1, 2, 3):
        there = step(y, d, NX)
        cp.start(q_ids[d], qsv.at[there // 2], qa.at[c, y], device_of(x, there, c, z))
    qa[c, y] = qsv[mine]
    across((0, 0))

    lane = lax.broadcasted_iota(jnp.int32, (T, W), 1)

    def split_heads(t, rows):
        marks = jnp.where(lane // 3 == t, 1.0, 0.0).astype(BF16)
        for h in range(2):
            qe[t, h, :, 0:W] = jnp.where(lane // 64 == h, rows, 0.0).astype(BF16)
            qe[t, h, :, W : 2 * W] = marks

    split_heads(0, jnp.where(open_all, qsv[0].astype(F32), qsv[1].astype(F32)))
    stat[...] = jnp.full(stat.shape, 2.0 * NEG, F32)
    acc[...] = jnp.zeros(acc.shape, F32)
    ones = jnp.ones((16, T), BF16)

    def fill(t, h, first, buf):
        top = None
        for j in range(CHUNK):
            slot = first + j
            k = jnp.concatenate([kv[slot, e, W : 2 * W] for e in range(2)], axis=0)
            s = nt(jnp.concatenate([k, ext[slot]], axis=1), qe[t, h])
            buf[j] = s
            top = s if top is None else jnp.maximum(top, s)
        return jnp.max(top, axis=0, keepdims=True)

    def absorb(t, h, first, buf, top):
        old = stat[t, h, 0:1]
        new = jnp.maximum(old, top)
        factor = jnp.exp(old - new)
        stat[t, h, 0:1] = new
        added = None
        for j in range(CHUNK):
            p = jnp.exp(buf[j] - new).astype(BF16)
            values = jnp.concatenate([kv[first + j, e, pl.ds(h * 64, 64)] for e in range(2)], axis=1)
            values = jnp.concatenate([values, ones], axis=0)
            term = dot(values, p)
            added = term if added is None else added + term
        acc[t, h] = acc[t, h] * factor + added

    def attend(t, first, chunks):
        last = first + (chunks - 1) * CHUNK
        top = fill(t, 0, first, even)

        def one(i, top):
            at = first + i * CHUNK
            other = fill(t, 1, at, odd)
            absorb(t, 0, at, even, top)
            top = fill(t, 0, jnp.minimum(at + CHUNK, last), even)
            absorb(t, 1, at, odd, other)
            return top

        if chunks > 1:
            top = lax.fori_loop(0, chunks - 1, one, top)
        other = fill(t, 1, last, odd)
        absorb(t, 0, last, even, top)
        absorb(t, 1, last, odd, other)

    m_ids = [cp.new() for _ in range(NZ)]
    o_ids = [cp.new() for _ in range(NZ)]
    outward = (4, 3, 5, 2, 6, 1, 7)

    def part(i):
        return pl.ds(pl.multiple_of(i * PART, PART), PART)

    def finish(t):
        parts = [acc[t, h, 0:64] / acc[t, h, 64:65] for h in range(2)]
        mixed[t] = jnp.transpose(jnp.concatenate(parts, axis=0)).astype(BF16)

    def exchange():
        for d in outward:
            cp.start(m_ids[d], mixed.at[:, part(step(z, d, NZ))], rows_in.at[z], z_up(d))
        rows_in[z] = mixed[:, part(z)]

    def project():
        for d in range(1, NZ):
            cp.wait(m_ids[d], rows_in.at[step(z, -d, NZ)])
        rows = jnp.concatenate([rows_in[i].reshape(2 * PART, W) for i in range(NZ)], axis=1)
        product = dot(rows, wall[...].reshape(D, D)).astype(BF16)
        for i in range(NZ):
            rows_out[i] = product[:, i * W : (i + 1) * W].reshape(2, PART, W)
        for d in outward:
            cp.start(o_ids[d], rows_out.at[step(z, d, NZ)], done.at[z], z_up(d))
        done[z] = rows_out[z]

    def write():
        for d in range(1, NZ):
            cp.wait(o_ids[d], done.at[step(z, -d, NZ)])
        for i in range(NZ):
            for t in range(2):
                out[t, i * PART : (i + 1) * PART] = done[i, t]

    x_ids = [cp.new() for _ in range(4)]

    def select():
        for d in (1, 2, 3, 0):
            there = step(x, d, NX)
            g = group_of(there, y, c)
            for half in range(2):
                named = idx[:, pl.ds(pl.multiple_of(g * T + half * LANES, LANES), LANES)]
                named = jnp.transpose(jnp.broadcast_to(named, (LANES, LANES)))
                named = jnp.concatenate([named, named], axis=1)
                found = jnp.zeros((LANES, W), F32)
                for core in range(2):
                    for row in range(NX):
                        base = group_of(x, row, core) * T
                        here = named - base == lax.broadcasted_iota(jnp.int32, (LANES, T), 1)
                        found = found + dot(here.astype(F32).astype(BF16), qa[core, row])
                rows = pl.ds(half * LANES, LANES)
                if d:
                    qstage[d - 1, rows] = found.astype(BF16)
                else:
                    qx[x, rows] = found.astype(BF16)
            if d:
                cp.start(x_ids[d], qstage.at[d - 1], qx.at[x], device_of(there, y, c, z))

    u_hop(0)
    v_hop(0, 0)
    u_hop(1)
    for d in (1, 2, 3):
        cp.wait(q_ids[d], qa.at[c, step(y, -d, NX)])
    cp.start(q_ids[0], qa.at[c], qa.at[c], sibling)
    v_hop(1, 0)
    across((3, 0), (1, 0), (2, 0))
    for du in (3, 1, 2):
        v_hop(0, du)
    attend(0, 0, 1)
    v_rest(0)
    for du in (3, 1, 2):
        v_hop(1, du)
    cp.wait(q_ids[0], qa.at[1 - c])
    select()
    w_forward()
    w_near()
    w_across(1, 2, 6, 7)
    for du in (3, 1, 2):
        v_rest(du)
    v_end(0)
    attend(0, 4, 2)
    for du in (3, 1, 2):
        v_end(du)
    for d in (1, 2, 3):
        cp.wait(x_ids[d], qx.at[step(x, -d, NX)])
    split_heads(1, sum(qx[i].astype(F32) for i in range(NX)))
    attend(1, 0, 3)
    attend(0, 12, 1)
    attend(1, 12, 1)
    from_sibling(0, 8)
    attend(0, 16, 2)
    attend(1, 16, 2)
    w_end()
    w_across(3, 4, 5)
    from_sibling(8, 4)
    attend(0, 24, 1)
    attend(1, 24, 1)
    from_sibling(12, 4)
    attend(0, 28, 1)
    attend(1, 28, 1)
    finish(0)
    finish(1)
    exchange()
    w_wait()
    cp.drain(len(cp.sent) - len(outward))
    project()
    cp.drain(len(outward))
    write()
    cp.drain(len(outward))


def shards(points, anchor_index, tile_branch, norm_gain, q_surface, q_volume, kv_weight, out_weight):
    vmem = pl.BlockSpec(memory_space=pltpu.VMEM)
    anywhere = pl.BlockSpec(memory_space=pl.ANY)
    smem = pl.BlockSpec(memory_space=pltpu.SMEM)
    both = pl.pallas_call(
        kernel,
        out_shape=jax.ShapeDtypeStruct((2, T, W), BF16),
        in_specs=[anywhere, anywhere, smem, anywhere, anywhere, anywhere, anywhere, anywhere],
        out_specs=vmem,
        scratch_shapes=[
            pltpu.VMEM((1, G * T), jnp.int32),
            pltpu.VMEM((1, D), F32),
            pltpu.VMEM((2, NZ, H, W), BF16),
            pltpu.VMEM((2, H, D), BF16),
            pltpu.VMEM((D, W), BF16),
            pltpu.VMEM((D, W), BF16),
            pltpu.VMEM((2, D, W), BF16),
            pltpu.VMEM((NZ, 2, W // 2, D), BF16),
            pltpu.VMEM((G, 2, 2 * W, H), BF16),
            pltpu.VMEM((G, T, LANES), BF16),
            pltpu.VMEM((8, 64, LANES), F32),
            pltpu.VMEM((2, T, W), BF16),
            pltpu.VMEM((2, NX, T, W), BF16),
            pltpu.VMEM((NX, T, W), BF16),
            pltpu.VMEM((3, T, W), BF16),
            pltpu.VMEM((2, 2, T, 2 * W), BF16),
            pltpu.VMEM((2, 2, 8, T), F32),
            pltpu.VMEM((2, 2, 80, T), F32),
            pltpu.VMEM((CHUNK, T, T), F32),
            pltpu.VMEM((CHUNK, T, T), F32),
            pltpu.VMEM((2, T, W), BF16),
            pltpu.VMEM((NZ, 2, PART, W), BF16),
            pltpu.VMEM((NZ, 2, PART, W), BF16),
            pltpu.VMEM((NZ, 2, PART, W), BF16),
            pltpu.SemaphoreType.DMA((9,)),
            pltpu.SemaphoreType.DMA((N_COPIES,)),
            pltpu.SemaphoreType.DMA((N_COPIES,)),
        ],
        compiler_params=pltpu.CompilerParams(
            collective_id=0, has_side_effects=True, vmem_limit_bytes=60 * 1024 * 1024
        ),
    )(
        points,
        anchor_index.reshape(1, -1),
        tile_branch,
        norm_gain.reshape(1, -1),
        q_surface,
        q_volume,
        kv_weight,
        out_weight,
    )
    return both[0], both[1]


def solution(mesh):
    in_specs = (
        P(("pt", "anc"), "head"),
        P(),
        P(("pt", "anc")),
        P(),
        P(None, "head"),
        P(None, "head"),
        P(None, None, "head"),
        P("head", None),
    )
    out_specs = (P(("pt", "anc"), "head"), P(("pt", "anc"), "head"))
    return jax.shard_map(shards, mesh=mesh, in_specs=in_specs, out_specs=out_specs, check_vma=False)
```

```python
import jax
import jax.numpy as jnp
from jax import lax
from jax.experimental import pallas as pl
from jax.experimental.pallas import tpu as pltpu
from jax.sharding import PartitionSpec as P

MESH = pl.DeviceIdType.MESH
F32 = jnp.float32
BF16 = jnp.bfloat16
NEG = -1e30
T = 256
W = 128
G = 32
NZ = 8
NX = 4
LANES = 128
D = 1024
N_COPIES = 128
H = T // 2
PART = T // NZ
CHUNK = 4
ORDER = (
    (0, 0), (3, 0), (1, 0), (2, 0),
    (0, 3), (0, 1), (3, 3), (3, 1),
    (1, 3), (1, 1), (2, 3), (2, 1),
    (0, 2), (3, 2), (1, 2), (2, 2),
)
SLOT = {pair: i for i, pair in enumerate(ORDER)}


def group_of(x, y, c):
    return y * 8 + lax.rem(x, 2) * 4 + c * 2 + x // 2


def device_of(x, y, c, z):
    return (y * 4 + lax.rem(x, 2) * 2 + c, x // 2, z)


def nt(a, b):
    return lax.dot_general(a, b, (((1,), (1,)), ((), ())), preferred_element_type=F32)


def dot(a, b):
    return jnp.dot(a, b, preferred_element_type=F32)


class Copies:
    def __init__(self, send, recv, home):
        self.send, self.recv, self.home, self.count, self.sent = send, recv, home, 0, []

    def new(self):
        self.count += 1
        return self.count - 1

    def make(self, k, src, dst, device):
        return pltpu.make_async_remote_copy(
            src_ref=src,
            dst_ref=dst,
            send_sem=self.send.at[k],
            recv_sem=self.recv.at[k],
            device_id=device,
            device_id_type=MESH,
        )

    def start(self, k, src, dst, device):
        copy = self.make(k, src, dst, device)
        copy.start()
        self.sent.append(copy)

    def wait(self, k, landed):
        self.make(k, landed, landed, self.home).wait_recv()

    def drain(self, count):
        for copy in self.sent[:count]:
            copy.wait_send()
        self.sent = self.sent[count:]


def kernel(
    points, idx_in, branch, gain_in, wqs, wqv, wkv, wo,
    out,
    idx, gain, gp, nrm, vqs, vqv, vkv, wall, kv, ext, logs, qsv, qa, qx, qstage, qe,
    stat, acc, even, odd, mixed, rows_in, rows_out, done,
    wsem, send, recv,
):
    pt, anc, z = lax.axis_index("pt"), lax.axis_index("anc"), lax.axis_index("head")
    c = lax.rem(pt, 2)
    x = anc * 2 + lax.rem(pt // 2, 2)
    y = pt // 4
    cp = Copies(send, recv, (pt, anc, z))

    def step(i, d, n):
        return lax.rem(i + d + n, n)

    peers = [device_of(x, y, c, step(z, d, NZ)) for d in range(1, NZ)]
    peers += [device_of(step(x, d, NX), y, c, z) for d in range(1, NX)]
    peers += [device_of(x, step(y, d, NX), c, z) for d in range(1, NX)]
    sibling = device_of(x, y, 1 - c, z)
    peers += [sibling]
    barrier = pltpu.get_barrier_semaphore()
    for peer in peers:
        pl.semaphore_signal(barrier, inc=1, device_id=peer, device_id_type=MESH)

    pairs = (
        (points.at[pl.ds(0, H)], gp.at[0, z]), (points.at[pl.ds(H, H)], gp.at[1, z]), (idx_in, idx), (gain_in, gain),
        (wkv, vkv), (wqs, vqs), (wqv, vqv),
        (wo.at[pl.ds(0, W // 2)], wall.at[z, 0]), (wo.at[pl.ds(W // 2, W // 2)], wall.at[z, 1]),
    )
    loads = [pltpu.make_async_copy(src, dst, wsem.at[i]) for i, (src, dst) in enumerate(pairs)]
    for load in loads:
        load.start()
    loads[0].wait()
    loads[1].wait()
    pl.semaphore_wait(barrier, len(peers))

    def z_up(d):
        return device_of(x, y, c, step(z, d, NZ))


    def z_gather(at, rows):
        ids = [cp.new() for _ in range(8)]
        first, second = pl.ds(0, rows // 2), pl.ds(rows // 2, rows // 2)

        def begin():
            for k, d in enumerate((2, -2, 1, -1)):
                cp.start(ids[k], at(z), at(z), z_up(d))

        def forward():
            here = at(step(z, -2, NZ))
            cp.wait(ids[0], here)
            cp.start(ids[4], here, here, z_up(1))
            cp.start(ids[6], here.at[first], here.at[first], z_up(2))
            here = at(step(z, 2, NZ))
            cp.wait(ids[1], here)
            cp.start(ids[5], here, here, z_up(-1))
            cp.start(ids[7], here.at[second], here.at[second], z_up(-2))

        def near():
            cp.wait(ids[2], at(step(z, -1, NZ)))
            cp.wait(ids[3], at(step(z, 1, NZ)))

        def end():
            cp.wait(ids[4], at(step(z, -3, NZ)))
            cp.wait(ids[5], at(step(z, 3, NZ)))
            here = at(step(z, 4, NZ))
            cp.wait(ids[6], here.at[first])
            cp.wait(ids[7], here.at[second])

        return begin, forward, near, end

    halves = [z_gather(lambda i, e=e: gp.at[e, i], H) for e in range(2)]
    for begin, _, _, _ in halves:
        begin()

    def tally(first, count):
        total = jnp.zeros((64, LANES), F32)
        for i in range(count):
            row = idx[:, pl.ds((first + i) * 1024, 1024)]
            upper = (row // 128 == lax.broadcasted_iota(jnp.int32, (64, 1024), 0)).astype(F32)
            lower = (lax.rem(row, 128) == lax.broadcasted_iota(jnp.int32, (128, 1024), 0)).astype(F32)
            total = total + nt(upper.astype(BF16), lower.astype(BF16))
        return total

    loads[2].wait()
    surface = tally(0, 4)
    volume = tally(4, 4)
    everyone = surface + volume
    open_all = branch[0] == 1

    def log_count(n):
        return jnp.where(n > 0.0, jnp.log(jnp.maximum(n, 1.0)), NEG)

    for t, n in enumerate((jnp.where(open_all, everyone, volume), everyone)):
        rest = log_count(n)
        for j in range(3):
            term = rest.astype(BF16).astype(F32)
            logs[3 * t + j] = term
            rest = rest - term
    for _, forward, _, _ in halves:
        forward()

    u, v = (1 - c) * x + c * y, (1 - c) * y + c * x

    def place(i, j):
        return (1 - c) * i + c * j, (1 - c) * j + c * i

    def group_at(slot):
        du, dv = ORDER[slot % 16]
        if slot < 16:
            bx, by = place(step(u, du, NX), step(v, dv, NX))
            return group_of(bx, by, c)
        bx, by = place(step(u, dv, NX), step(v, du, NX))
        return group_of(bx, by, 1 - c)

    sub = lax.broadcasted_iota(jnp.int32, (8, LANES), 0)
    for slot in range(G):
        g = group_at(slot)
        for half in range(2):
            terms = jnp.zeros((8, LANES), F32)
            for j in range(6):
                terms = jnp.where(sub == j, logs[j, pl.ds(2 * g + half, 1)], terms)
            terms = jnp.concatenate([terms, jnp.zeros((LANES - 8, LANES), F32)], axis=0)
            ext[slot, pl.ds(half * LANES, LANES)] = jnp.transpose(terms).astype(BF16)

    for load in loads[3:]:
        load.wait()

    def project_half(e):
        total = jnp.zeros((H, LANES), F32)
        for i in range(NZ):
            part = gp[e, i].astype(F32)
            total = total + part * part
        scale = lax.rsqrt(jnp.sum(total, axis=-1, keepdims=True) * (1.0 / D) + 1e-06)
        for i in range(NZ):
            columns = pl.ds(i * W, W)
            nrm[e, :, columns] = (gp[e, i].astype(F32) * scale * gain[:, columns]).astype(BF16)
        kv[0, e, W : 2 * W] = dot(nrm[e], vkv[0]).astype(BF16)
        kv[0, e, 0:W] = jnp.transpose(dot(nrm[e], vkv[1])).astype(BF16)

    def toward(du, dv):
        bx, by = place(step(u, du, NX), step(v, dv, NX))
        return device_of(bx, by, c, z)

    u_ids = [[cp.new() for _ in range(3)] for _ in range(2)]
    v_ids = [[[cp.new() for _ in range(3)] for _ in range(4)] for _ in range(2)]
    s_ids = [cp.new() for _ in range(16)]

    def pass_on(k, e, src, dst, device):
        cp.start(k, kv.at[SLOT[src], e], kv.at[SLOT[dst], e], device)

    def landed(k, e, pair):
        cp.wait(k, kv.at[SLOT[pair], e])

    def share(e, du):
        pass_on(v_ids[e][du][0], e, (du, 0), (du, 3), toward(0, 1))
        pass_on(v_ids[e][du][1], e, (du, 0), (du, 1), toward(0, -1))

    def across(*pairs):
        for pair in pairs:
            slot = SLOT[pair]
            cp.start(s_ids[slot], kv.at[slot], kv.at[16 + slot], sibling)

    def from_sibling(first, count):
        for slot in range(first, first + count):
            cp.wait(s_ids[slot], kv.at[16 + slot])

    def kv_begin(e):
        pass_on(u_ids[e][0], e, (0, 0), (3, 0), toward(1, 0))
        pass_on(u_ids[e][1], e, (0, 0), (1, 0), toward(-1, 0))
        share(e, 0)
        pass_on(u_ids[e][2], e, (0, 0), (2, 0), toward(2, 0))

    def u_hop(e):
        for k, du in ((0, 3), (1, 1), (2, 2)):
            landed(u_ids[e][k], e, (du, 0))
            share(e, du)

    def v_hop(e, du):
        landed(v_ids[e][du][e], e, (du, 3 - 2 * e))
        pass_on(v_ids[e][du][2], e, (du, 3 - 2 * e), (du, 2), toward(0, 1 - 2 * e))

    def v_rest(du):
        landed(v_ids[1][du][0], 1, (du, 3))
        landed(v_ids[0][du][1], 0, (du, 1))
        across((du, 3), (du, 1))

    def v_end(du):
        landed(v_ids[0][du][2], 0, (du, 2))
        landed(v_ids[1][du][2], 1, (du, 2))
        across((du, 2))

    mine = y // 2
    q_ids = [[cp.new() for _ in range(4)] for _ in range(2)]

    def queries(e):
        rows = pl.ds(e * H, H)
        qsv[0, rows] = dot(nrm[e], vqs[...]).astype(BF16) * BF16(0.125)
        qsv[1, rows] = dot(nrm[e], vqv[...]).astype(BF16) * BF16(0.125)
        for d in (1, 2, 3):
            there = step(y, d, NX)
            cp.start(q_ids[e][d], qsv.at[there // 2, rows], qa.at[c, y, rows], device_of(x, there, c, z))
        qa[c, y, rows] = qsv[mine, rows]

    def q_across():
        for e in range(2):
            for d in (1, 2, 3):
                cp.wait(q_ids[e][d], qa.at[c, step(y, -d, NX), pl.ds(e * H, H)])
        cp.start(q_ids[0][0], qa.at[c], qa.at[c], sibling)

    halves[0][2]()
    halves[0][3]()
    project_half(0)
    kv_begin(0)
    queries(0)
    halves[1][2]()
    halves[1][3]()
    w_begin, w_forward, w_near, w_end = z_gather(lambda i: wall.at[i, c], W // 2)
    w_ids = [cp.new() for _ in range(NZ)]

    def w_across(*distances):
        for d in distances:
            at = step(z, d, NZ)
            cp.start(w_ids[d], wall.at[at, c], wall.at[at, c], sibling)

    def w_wait():
        for d in range(1, NZ):
            cp.wait(w_ids[d], wall.at[step(z, d, NZ), 1 - c])

    w_begin()
    project_half(1)
    kv_begin(1)
    queries(1)
    across((0, 0))

    lane = lax.broadcasted_iota(jnp.int32, (T, W), 1)

    def split_heads(t, rows):
        marks = jnp.where(lane // 3 == t, 1.0, 0.0).astype(BF16)
        for h in range(2):
            qe[t, h, :, 0:W] = jnp.where(lane // 64 == h, rows, 0.0).astype(BF16)
            qe[t, h, :, W : 2 * W] = marks

    split_heads(0, jnp.where(open_all, qsv[0].astype(F32), qsv[1].astype(F32)))
    stat[...] = jnp.full(stat.shape, 2.0 * NEG, F32)
    acc[...] = jnp.zeros(acc.shape, F32)
    ones = jnp.ones((16, T), BF16)

    def fill(t, h, first, buf):
        top = None
        for j in range(CHUNK):
            slot = first + j
            k = jnp.concatenate([kv[slot, e, W : 2 * W] for e in range(2)], axis=0)
            s = nt(jnp.concatenate([k, ext[slot]], axis=1), qe[t, h])
            buf[j] = s
            top = s if top is None else jnp.maximum(top, s)
        return jnp.max(top, axis=0, keepdims=True)

    def absorb(t, h, first, buf, top):
        old = stat[t, h, 0:1]
        new = jnp.maximum(old, top)
        factor = jnp.exp(old - new)
        stat[t, h, 0:1] = new
        added = None
        for j in range(CHUNK):
            p = jnp.exp(buf[j] - new).astype(BF16)
            values = jnp.concatenate([kv[first + j, e, pl.ds(h * 64, 64)] for e in range(2)], axis=1)
            values = jnp.concatenate([values, ones], axis=0)
            term = dot(values, p)
            added = term if added is None else added + term
        acc[t, h] = acc[t, h] * factor + added

    def attend(t, first, chunks):
        last = first + (chunks - 1) * CHUNK
        top = fill(t, 0, first, even)

        def one(i, top):
            at = first + i * CHUNK
            other = fill(t, 1, at, odd)
            absorb(t, 0, at, even, top)
            top = fill(t, 0, jnp.minimum(at + CHUNK, last), even)
            absorb(t, 1, at, odd, other)
            return top

        if chunks > 1:
            top = lax.fori_loop(0, chunks - 1, one, top)
        other = fill(t, 1, last, odd)
        absorb(t, 0, last, even, top)
        absorb(t, 1, last, odd, other)

    def attend_both(first):
        top = fill(0, 0, first, even)
        other = fill(0, 1, first, odd)
        absorb(0, 0, first, even, top)
        top = fill(1, 0, first, even)
        absorb(0, 1, first, odd, other)
        other = fill(1, 1, first, odd)
        absorb(1, 0, first, even, top)
        absorb(1, 1, first, odd, other)

    m_ids = [cp.new() for _ in range(NZ)]
    o_ids = [cp.new() for _ in range(NZ)]
    outward = (4, 3, 5, 2, 6, 1, 7)

    def part(i):
        return pl.ds(pl.multiple_of(i * PART, PART), PART)

    def finish(t):
        parts = [acc[t, h, 0:64] / acc[t, h, 64:65] for h in range(2)]
        mixed[t] = jnp.transpose(jnp.concatenate(parts, axis=0)).astype(BF16)

    def exchange():
        for d in outward:
            cp.start(m_ids[d], mixed.at[:, part(step(z, d, NZ))], rows_in.at[z], z_up(d))
        rows_in[z] = mixed[:, part(z)]

    def project():
        for d in range(1, NZ):
            cp.wait(m_ids[d], rows_in.at[step(z, -d, NZ)])
        rows = jnp.concatenate([rows_in[i].reshape(2 * PART, W) for i in range(NZ)], axis=1)
        product = dot(rows, wall[...].reshape(D, D)).astype(BF16)
        for i in range(NZ):
            rows_out[i] = product[:, i * W : (i + 1) * W].reshape(2, PART, W)
        for d in outward:
            cp.start(o_ids[d], rows_out.at[step(z, d, NZ)], done.at[z], z_up(d))
        done[z] = rows_out[z]

    def write():
        for d in range(1, NZ):
            cp.wait(o_ids[d], done.at[step(z, -d, NZ)])
        for i in range(NZ):
            for t in range(2):
                out[t, i * PART : (i + 1) * PART] = done[i, t]

    x_ids = [cp.new() for _ in range(4)]

    def select():
        for d in (1, 2, 3, 0):
            there = step(x, d, NX)
            g = group_of(there, y, c)
            for half in range(2):
                named = idx[:, pl.ds(pl.multiple_of(g * T + half * LANES, LANES), LANES)]
                named = jnp.transpose(jnp.broadcast_to(named, (LANES, LANES)))
                named = jnp.concatenate([named, named], axis=1)
                found = jnp.zeros((LANES, W), F32)
                for core in range(2):
                    for row in range(NX):
                        base = group_of(x, row, core) * T
                        here = named - base == lax.broadcasted_iota(jnp.int32, (LANES, T), 1)
                        found = found + dot(here.astype(F32).astype(BF16), qa[core, row])
                rows = pl.ds(half * LANES, LANES)
                if d:
                    qstage[d - 1, rows] = found.astype(BF16)
                else:
                    qx[x, rows] = found.astype(BF16)
            if d:
                cp.start(x_ids[d], qstage.at[d - 1], qx.at[x], device_of(there, y, c, z))

    u_hop(0)
    v_hop(0, 0)
    u_hop(1)
    q_across()
    v_hop(1, 0)
    across((3, 0), (1, 0), (2, 0))
    for du in (3, 1, 2):
        v_hop(0, du)
    attend(0, 0, 1)
    v_rest(0)
    for du in (3, 1, 2):
        v_hop(1, du)
    cp.wait(q_ids[0][0], qa.at[1 - c])
    select()
    for du in (3, 1, 2):
        v_rest(du)
    v_end(0)
    attend(0, 4, 2)
    for du in (3, 1, 2):
        v_end(du)
    from_sibling(0, 8)
    w_forward()
    w_near()
    w_across(1, 2, 6, 7)
    attend(0, 12, 3)
    for d in (1, 2, 3):
        cp.wait(x_ids[d], qx.at[step(x, -d, NX)])
    split_heads(1, sum(qx[i].astype(F32) for i in range(NX)))
    attend(1, 0, 6)

    def last(i, carry):
        for k in range(CHUNK):
            slot = 8 + i * CHUNK + k
            cp.wait(s_ids[0] + slot, kv.at[16 + slot])
        attend_both(24 + i * CHUNK)
        return carry

    lax.fori_loop(0, 2, last, 0)
    w_end()
    w_across(3, 4, 5)
    finish(0)
    finish(1)
    exchange()
    w_wait()
    cp.drain(len(cp.sent) - len(outward))
    project()
    cp.drain(len(outward))
    write()
    cp.drain(len(outward))


def shards(points, anchor_index, tile_branch, norm_gain, q_surface, q_volume, kv_weight, out_weight):
    vmem = pl.BlockSpec(memory_space=pltpu.VMEM)
    anywhere = pl.BlockSpec(memory_space=pl.ANY)
    smem = pl.BlockSpec(memory_space=pltpu.SMEM)
    both = pl.pallas_call(
        kernel,
        out_shape=jax.ShapeDtypeStruct((2, T, W), BF16),
        in_specs=[anywhere, anywhere, smem, anywhere, anywhere, anywhere, anywhere, anywhere],
        out_specs=vmem,
        scratch_shapes=[
            pltpu.VMEM((1, G * T), jnp.int32),
            pltpu.VMEM((1, D), F32),
            pltpu.VMEM((2, NZ, H, W), BF16),
            pltpu.VMEM((2, H, D), BF16),
            pltpu.VMEM((D, W), BF16),
            pltpu.VMEM((D, W), BF16),
            pltpu.VMEM((2, D, W), BF16),
            pltpu.VMEM((NZ, 2, W // 2, D), BF16),
            pltpu.VMEM((G, 2, 2 * W, H), BF16),
            pltpu.VMEM((G, T, LANES), BF16),
            pltpu.VMEM((8, 64, LANES), F32),
            pltpu.VMEM((2, T, W), BF16),
            pltpu.VMEM((2, NX, T, W), BF16),
            pltpu.VMEM((NX, T, W), BF16),
            pltpu.VMEM((3, T, W), BF16),
            pltpu.VMEM((2, 2, T, 2 * W), BF16),
            pltpu.VMEM((2, 2, 8, T), F32),
            pltpu.VMEM((2, 2, 80, T), F32),
            pltpu.VMEM((CHUNK, T, T), F32),
            pltpu.VMEM((CHUNK, T, T), F32),
            pltpu.VMEM((2, T, W), BF16),
            pltpu.VMEM((NZ, 2, PART, W), BF16),
            pltpu.VMEM((NZ, 2, PART, W), BF16),
            pltpu.VMEM((NZ, 2, PART, W), BF16),
            pltpu.SemaphoreType.DMA((9,)),
            pltpu.SemaphoreType.DMA((N_COPIES,)),
            pltpu.SemaphoreType.DMA((N_COPIES,)),
        ],
        compiler_params=pltpu.CompilerParams(
            collective_id=0, has_side_effects=True, vmem_limit_bytes=60 * 1024 * 1024
        ),
    )(
        points,
        anchor_index.reshape(1, -1),
        tile_branch,
        norm_gain.reshape(1, -1),
        q_surface,
        q_volume,
        kv_weight,
        out_weight,
    )
    return both[0], both[1]


def solution(mesh):
    in_specs = (
        P(("pt", "anc"), "head"),
        P(),
        P(("pt", "anc")),
        P(),
        P(None, "head"),
        P(None, "head"),
        P(None, None, "head"),
        P("head", None),
    )
    out_specs = (P(("pt", "anc"), "head"), P(("pt", "anc"), "head"))
    return jax.shard_map(shards, mesh=mesh, in_specs=in_specs, out_specs=out_specs, check_vma=False)
```

```python
import jax
import jax.numpy as jnp
from jax import lax
from jax.experimental import pallas as pl
from jax.experimental.pallas import tpu as pltpu
from jax.sharding import PartitionSpec as P

MESH = pl.DeviceIdType.MESH
F32 = jnp.float32
BF16 = jnp.bfloat16
NEG = -1e30
T = 256
W = 128
G = 32
NZ = 8
NX = 4
LANES = 128
D = 1024
N_COPIES = 128
H = T // 2
PART = T // NZ
CHUNK = 4
ORDER = (
    (0, 0), (3, 0), (1, 0), (2, 0),
    (0, 3), (0, 1), (3, 3), (3, 1),
    (1, 3), (1, 1), (2, 3), (2, 1),
    (0, 2), (3, 2), (1, 2), (2, 2),
)
SLOT = {pair: i for i, pair in enumerate(ORDER)}


def group_of(x, y, c):
    return y * 8 + lax.rem(x, 2) * 4 + c * 2 + x // 2


def device_of(x, y, c, z):
    return (y * 4 + lax.rem(x, 2) * 2 + c, x // 2, z)


def nt(a, b):
    return lax.dot_general(a, b, (((1,), (1,)), ((), ())), preferred_element_type=F32)


def dot(a, b):
    return jnp.dot(a, b, preferred_element_type=F32)


class Copies:
    def __init__(self, send, recv, home):
        self.send, self.recv, self.home, self.count, self.sent = send, recv, home, 0, []

    def new(self):
        self.count += 1
        return self.count - 1

    def make(self, k, src, dst, device):
        return pltpu.make_async_remote_copy(
            src_ref=src,
            dst_ref=dst,
            send_sem=self.send.at[k],
            recv_sem=self.recv.at[k],
            device_id=device,
            device_id_type=MESH,
        )

    def start(self, k, src, dst, device):
        copy = self.make(k, src, dst, device)
        copy.start()
        self.sent.append(copy)

    def wait(self, k, landed):
        self.make(k, landed, landed, self.home).wait_recv()

    def drain(self, count):
        for copy in self.sent[:count]:
            copy.wait_send()
        self.sent = self.sent[count:]


def kernel(
    points, idx_in, branch, gain_in, wqs, wqv, wkv, wo,
    out,
    idx, gain, gp, nrm, vqs, vqv, vkv, wall, kv, ext, logs, qsv, qa, qx, qstage, qe,
    stat, acc, even, odd, mixed, rows_in, rows_out, done,
    wsem, send, recv,
):
    pt, anc, z = lax.axis_index("pt"), lax.axis_index("anc"), lax.axis_index("head")
    c = lax.rem(pt, 2)
    x = anc * 2 + lax.rem(pt // 2, 2)
    y = pt // 4
    cp = Copies(send, recv, (pt, anc, z))

    def step(i, d, n):
        return lax.rem(i + d + n, n)

    peers = [device_of(x, y, c, step(z, d, NZ)) for d in range(1, NZ)]
    peers += [device_of(step(x, d, NX), y, c, z) for d in range(1, NX)]
    peers += [device_of(x, step(y, d, NX), c, z) for d in range(1, NX)]
    sibling = device_of(x, y, 1 - c, z)
    peers += [sibling]
    pairs = (
        (points.at[pl.ds(0, H)], gp.at[0, z]), (points.at[pl.ds(H, H)], gp.at[1, z]), (idx_in, idx), (gain_in, gain),
        (wkv, vkv), (wqs, vqs), (wqv, vqv),
        (wo.at[pl.ds(0, W // 2)], wall.at[z, 0]), (wo.at[pl.ds(W // 2, W // 2)], wall.at[z, 1]),
    )
    loads = [pltpu.make_async_copy(src, dst, wsem.at[i]) for i, (src, dst) in enumerate(pairs)]
    for load in loads:
        load.start()
    barrier = pltpu.get_barrier_semaphore()
    for peer in peers:
        pl.semaphore_signal(barrier, inc=1, device_id=peer, device_id_type=MESH)

    loads[0].wait()
    loads[1].wait()
    pl.semaphore_wait(barrier, len(peers))

    def z_up(d):
        return device_of(x, y, c, step(z, d, NZ))


    def z_gather(at, rows):
        ids = [cp.new() for _ in range(8)]
        first, second = pl.ds(0, rows // 2), pl.ds(rows // 2, rows // 2)

        def begin():
            for k, d in enumerate((2, -2, 1, -1)):
                cp.start(ids[k], at(z), at(z), z_up(d))

        def forward():
            here = at(step(z, -2, NZ))
            cp.wait(ids[0], here)
            cp.start(ids[4], here, here, z_up(1))
            cp.start(ids[6], here.at[first], here.at[first], z_up(2))
            here = at(step(z, 2, NZ))
            cp.wait(ids[1], here)
            cp.start(ids[5], here, here, z_up(-1))
            cp.start(ids[7], here.at[second], here.at[second], z_up(-2))

        def near():
            cp.wait(ids[2], at(step(z, -1, NZ)))
            cp.wait(ids[3], at(step(z, 1, NZ)))

        def end():
            cp.wait(ids[4], at(step(z, -3, NZ)))
            cp.wait(ids[5], at(step(z, 3, NZ)))
            here = at(step(z, 4, NZ))
            cp.wait(ids[6], here.at[first])
            cp.wait(ids[7], here.at[second])

        return begin, forward, near, end

    halves = [z_gather(lambda i, e=e: gp.at[e, i], H) for e in range(2)]
    for begin, _, _, _ in halves:
        begin()

    def tally(first, count):
        total = jnp.zeros((64, LANES), F32)
        for i in range(count):
            row = idx[:, pl.ds((first + i) * 1024, 1024)]
            upper = (row // 128 == lax.broadcasted_iota(jnp.int32, (64, 1024), 0)).astype(F32)
            lower = (lax.rem(row, 128) == lax.broadcasted_iota(jnp.int32, (128, 1024), 0)).astype(F32)
            total = total + nt(upper.astype(BF16), lower.astype(BF16))
        return total

    loads[2].wait()
    surface = tally(0, 4)
    volume = tally(4, 4)
    everyone = surface + volume
    open_all = branch[0] == 1

    def log_count(n):
        return jnp.where(n > 0.0, jnp.log(jnp.maximum(n, 1.0)), NEG)

    for t, n in enumerate((jnp.where(open_all, everyone, volume), everyone)):
        rest = log_count(n)
        for j in range(3):
            term = rest.astype(BF16).astype(F32)
            logs[3 * t + j] = term
            rest = rest - term
    for _, forward, _, _ in halves:
        forward()

    u, v = (1 - c) * x + c * y, (1 - c) * y + c * x

    def place(i, j):
        return (1 - c) * i + c * j, (1 - c) * j + c * i

    def group_at(slot):
        du, dv = ORDER[slot % 16]
        if slot < 16:
            bx, by = place(step(u, du, NX), step(v, dv, NX))
            return group_of(bx, by, c)
        bx, by = place(step(u, dv, NX), step(v, du, NX))
        return group_of(bx, by, 1 - c)

    sub = lax.broadcasted_iota(jnp.int32, (8, LANES), 0)
    for slot in range(G):
        g = group_at(slot)
        for half in range(2):
            terms = jnp.zeros((8, LANES), F32)
            for j in range(6):
                terms = jnp.where(sub == j, logs[j, pl.ds(2 * g + half, 1)], terms)
            terms = jnp.concatenate([terms, jnp.zeros((LANES - 8, LANES), F32)], axis=0)
            ext[slot, pl.ds(half * LANES, LANES)] = jnp.transpose(terms).astype(BF16)

    for load in loads[3:]:
        load.wait()

    def project_half(e):
        total = jnp.zeros((H, LANES), F32)
        for i in range(NZ):
            part = gp[e, i].astype(F32)
            total = total + part * part
        scale = lax.rsqrt(jnp.sum(total, axis=-1, keepdims=True) * (1.0 / D) + 1e-06)
        for i in range(NZ):
            columns = pl.ds(i * W, W)
            nrm[e, :, columns] = (gp[e, i].astype(F32) * scale * gain[:, columns]).astype(BF16)
        kv[0, e, W : 2 * W] = dot(nrm[e], vkv[0]).astype(BF16)
        kv[0, e, 0:W] = jnp.transpose(dot(nrm[e], vkv[1])).astype(BF16)

    def toward(du, dv):
        bx, by = place(step(u, du, NX), step(v, dv, NX))
        return device_of(bx, by, c, z)

    u_ids = [[cp.new() for _ in range(3)] for _ in range(2)]
    v_ids = [[[cp.new() for _ in range(3)] for _ in range(4)] for _ in range(2)]
    s_ids = [cp.new() for _ in range(16)]

    def pass_on(k, e, src, dst, device):
        cp.start(k, kv.at[SLOT[src], e], kv.at[SLOT[dst], e], device)

    def landed(k, e, pair):
        cp.wait(k, kv.at[SLOT[pair], e])

    def share(e, du):
        pass_on(v_ids[e][du][0], e, (du, 0), (du, 3), toward(0, 1))
        pass_on(v_ids[e][du][1], e, (du, 0), (du, 1), toward(0, -1))

    def across(*pairs):
        for pair in pairs:
            slot = SLOT[pair]
            cp.start(s_ids[slot], kv.at[slot], kv.at[16 + slot], sibling)

    def from_sibling(first, count):
        for slot in range(first, first + count):
            cp.wait(s_ids[slot], kv.at[16 + slot])

    def kv_begin(e):
        pass_on(u_ids[e][0], e, (0, 0), (3, 0), toward(1, 0))
        pass_on(u_ids[e][1], e, (0, 0), (1, 0), toward(-1, 0))
        share(e, 0)
        pass_on(u_ids[e][2], e, (0, 0), (2, 0), toward(2, 0))

    def u_hop(e):
        for k, du in ((0, 3), (1, 1), (2, 2)):
            landed(u_ids[e][k], e, (du, 0))
            share(e, du)

    def v_hop(e, du):
        landed(v_ids[e][du][e], e, (du, 3 - 2 * e))
        pass_on(v_ids[e][du][2], e, (du, 3 - 2 * e), (du, 2), toward(0, 1 - 2 * e))

    def v_rest(du):
        landed(v_ids[1][du][0], 1, (du, 3))
        landed(v_ids[0][du][1], 0, (du, 1))
        across((du, 3), (du, 1))

    def v_end(du):
        landed(v_ids[0][du][2], 0, (du, 2))
        landed(v_ids[1][du][2], 1, (du, 2))
        across((du, 2))

    mine = y // 2
    q_ids = [[cp.new() for _ in range(4)] for _ in range(2)]

    def queries(e):
        rows = pl.ds(e * H, H)
        qsv[0, rows] = dot(nrm[e], vqs[...]).astype(BF16) * BF16(0.125)
        qsv[1, rows] = dot(nrm[e], vqv[...]).astype(BF16) * BF16(0.125)
        for d in (1, 2, 3):
            there = step(y, d, NX)
            cp.start(q_ids[e][d], qsv.at[there // 2, rows], qa.at[c, y, rows], device_of(x, there, c, z))
        qa[c, y, rows] = qsv[mine, rows]

    def q_across():
        for e in range(2):
            for d in (1, 2, 3):
                cp.wait(q_ids[e][d], qa.at[c, step(y, -d, NX), pl.ds(e * H, H)])
        cp.start(q_ids[0][0], qa.at[c], qa.at[c], sibling)

    halves[0][2]()
    halves[0][3]()
    project_half(0)
    kv_begin(0)
    queries(0)
    halves[1][2]()
    halves[1][3]()
    w_begin, w_forward, w_near, w_end = z_gather(lambda i: wall.at[i, c], W // 2)
    w_ids = [cp.new() for _ in range(NZ)]

    def w_across(*distances):
        for d in distances:
            at = step(z, d, NZ)
            cp.start(w_ids[d], wall.at[at, c], wall.at[at, c], sibling)

    def w_wait():
        for d in range(1, NZ):
            cp.wait(w_ids[d], wall.at[step(z, d, NZ), 1 - c])

    w_begin()
    project_half(1)
    kv_begin(1)
    queries(1)
    across((0, 0))

    lane = lax.broadcasted_iota(jnp.int32, (T, W), 1)

    def split_heads(t, rows):
        marks = jnp.where(lane // 3 == t, 1.0, 0.0).astype(BF16)
        for h in range(2):
            qe[t, h, :, 0:W] = jnp.where(lane // 64 == h, rows, 0.0).astype(BF16)
            qe[t, h, :, W : 2 * W] = marks

    split_heads(0, jnp.where(open_all, qsv[0].astype(F32), qsv[1].astype(F32)))
    stat[...] = jnp.full(stat.shape, 2.0 * NEG, F32)
    acc[...] = jnp.zeros(acc.shape, F32)
    ones = jnp.ones((16, T), BF16)

    def fill(t, h, first, buf):
        top = None
        for j in range(CHUNK):
            slot = first + j
            k = jnp.concatenate([kv[slot, e, W : 2 * W] for e in range(2)], axis=0)
            s = nt(jnp.concatenate([k, ext[slot]], axis=1), qe[t, h])
            buf[j] = s
            top = s if top is None else jnp.maximum(top, s)
        return jnp.max(top, axis=0, keepdims=True)

    def absorb(t, h, first, buf, top):
        old = stat[t, h, 0:1]
        new = jnp.maximum(old, top)
        factor = jnp.exp(old - new)
        stat[t, h, 0:1] = new
        added = None
        for j in range(CHUNK):
            p = jnp.exp(buf[j] - new).astype(BF16)
            values = jnp.concatenate([kv[first + j, e, pl.ds(h * 64, 64)] for e in range(2)], axis=1)
            values = jnp.concatenate([values, ones], axis=0)
            term = dot(values, p)
            added = term if added is None else added + term
        acc[t, h] = acc[t, h] * factor + added

    def attend(t, first, chunks):
        last = first + (chunks - 1) * CHUNK
        top = fill(t, 0, first, even)

        def one(i, top):
            at = first + i * CHUNK
            other = fill(t, 1, at, odd)
            absorb(t, 0, at, even, top)
            top = fill(t, 0, jnp.minimum(at + CHUNK, last), even)
            absorb(t, 1, at, odd, other)
            return top

        if chunks > 1:
            top = lax.fori_loop(0, chunks - 1, one, top)
        other = fill(t, 1, last, odd)
        absorb(t, 0, last, even, top)
        absorb(t, 1, last, odd, other)

    def attend_both(first):
        top = fill(0, 0, first, even)
        other = fill(0, 1, first, odd)
        absorb(0, 0, first, even, top)
        top = fill(1, 0, first, even)
        absorb(0, 1, first, odd, other)
        other = fill(1, 1, first, odd)
        absorb(1, 0, first, even, top)
        absorb(1, 1, first, odd, other)

    m_ids = [cp.new() for _ in range(NZ)]
    o_ids = [cp.new() for _ in range(NZ)]
    outward = (4, 3, 5, 2, 6, 1, 7)

    def part(i):
        return pl.ds(pl.multiple_of(i * PART, PART), PART)

    def finish(t):
        parts = [acc[t, h, 0:64] / acc[t, h, 64:65] for h in range(2)]
        mixed[t] = jnp.transpose(jnp.concatenate(parts, axis=0)).astype(BF16)

    def exchange():
        for d in outward:
            cp.start(m_ids[d], mixed.at[:, part(step(z, d, NZ))], rows_in.at[z], z_up(d))
        rows_in[z] = mixed[:, part(z)]

    def project():
        for d in range(1, NZ):
            cp.wait(m_ids[d], rows_in.at[step(z, -d, NZ)])
        rows = jnp.concatenate([rows_in[i].reshape(2 * PART, W) for i in range(NZ)], axis=1)
        product = dot(rows, wall[...].reshape(D, D)).astype(BF16)
        for i in range(NZ):
            rows_out[i] = product[:, i * W : (i + 1) * W].reshape(2, PART, W)
        for d in outward:
            cp.start(o_ids[d], rows_out.at[step(z, d, NZ)], done.at[z], z_up(d))
        done[z] = rows_out[z]

    def write():
        for d in range(1, NZ):
            cp.wait(o_ids[d], done.at[step(z, -d, NZ)])
        for i in range(NZ):
            for t in range(2):
                out[t, i * PART : (i + 1) * PART] = done[i, t]

    x_ids = [cp.new() for _ in range(4)]

    def select():
        for d in (1, 2, 3, 0):
            there = step(x, d, NX)
            g = group_of(there, y, c)
            for half in range(2):
                named = idx[:, pl.ds(pl.multiple_of(g * T + half * LANES, LANES), LANES)]
                named = jnp.transpose(jnp.broadcast_to(named, (LANES, LANES)))
                named = jnp.concatenate([named, named], axis=1)
                found = jnp.zeros((LANES, W), F32)
                for core in range(2):
                    for row in range(NX):
                        base = group_of(x, row, core) * T
                        here = named - base == lax.broadcasted_iota(jnp.int32, (LANES, T), 1)
                        found = found + dot(here.astype(F32).astype(BF16), qa[core, row])
                rows = pl.ds(half * LANES, LANES)
                if d:
                    qstage[d - 1, rows] = found.astype(BF16)
                else:
                    qx[x, rows] = found.astype(BF16)
            if d:
                cp.start(x_ids[d], qstage.at[d - 1], qx.at[x], device_of(there, y, c, z))

    u_hop(0)
    v_hop(0, 0)
    u_hop(1)
    q_across()
    v_hop(1, 0)
    across((3, 0), (1, 0), (2, 0))
    for du in (3, 1, 2):
        v_hop(0, du)
    attend(0, 0, 1)
    v_rest(0)
    for du in (3, 1, 2):
        v_hop(1, du)
    cp.wait(q_ids[0][0], qa.at[1 - c])
    select()
    for du in (3, 1, 2):
        v_rest(du)
    v_end(0)
    attend(0, 4, 2)
    for du in (3, 1, 2):
        v_end(du)
    from_sibling(0, 8)
    w_forward()
    w_near()
    w_across(1, 2, 6, 7)
    attend(0, 12, 3)
    for d in (1, 2, 3):
        cp.wait(x_ids[d], qx.at[step(x, -d, NX)])
    split_heads(1, sum(qx[i].astype(F32) for i in range(NX)))
    attend(1, 0, 6)

    def last(i, carry):
        for k in range(CHUNK):
            slot = 8 + i * CHUNK + k
            cp.wait(s_ids[0] + slot, kv.at[16 + slot])
        attend_both(24 + i * CHUNK)
        return carry

    lax.fori_loop(0, 2, last, 0)
    finish(0)
    finish(1)
    exchange()
    w_end()
    w_across(3, 4, 5)
    w_wait()
    cp.drain(len(cp.sent) - len(outward))
    project()
    cp.drain(len(outward))
    write()
    cp.drain(len(outward))


def shards(points, anchor_index, tile_branch, norm_gain, q_surface, q_volume, kv_weight, out_weight):
    vmem = pl.BlockSpec(memory_space=pltpu.VMEM)
    anywhere = pl.BlockSpec(memory_space=pl.ANY)
    smem = pl.BlockSpec(memory_space=pltpu.SMEM)
    both = pl.pallas_call(
        kernel,
        out_shape=jax.ShapeDtypeStruct((2, T, W), BF16),
        in_specs=[anywhere, anywhere, smem, anywhere, anywhere, anywhere, anywhere, anywhere],
        out_specs=vmem,
        scratch_shapes=[
            pltpu.VMEM((1, G * T), jnp.int32),
            pltpu.VMEM((1, D), F32),
            pltpu.VMEM((2, NZ, H, W), BF16),
            pltpu.VMEM((2, H, D), BF16),
            pltpu.VMEM((D, W), BF16),
            pltpu.VMEM((D, W), BF16),
            pltpu.VMEM((2, D, W), BF16),
            pltpu.VMEM((NZ, 2, W // 2, D), BF16),
            pltpu.VMEM((G, 2, 2 * W, H), BF16),
            pltpu.VMEM((G, T, LANES), BF16),
            pltpu.VMEM((8, 64, LANES), F32),
            pltpu.VMEM((2, T, W), BF16),
            pltpu.VMEM((2, NX, T, W), BF16),
            pltpu.VMEM((NX, T, W), BF16),
            pltpu.VMEM((3, T, W), BF16),
            pltpu.VMEM((2, 2, T, 2 * W), BF16),
            pltpu.VMEM((2, 2, 8, T), F32),
            pltpu.VMEM((2, 2, 80, T), F32),
            pltpu.VMEM((CHUNK, T, T), F32),
            pltpu.VMEM((CHUNK, T, T), F32),
            pltpu.VMEM((2, T, W), BF16),
            pltpu.VMEM((NZ, 2, PART, W), BF16),
            pltpu.VMEM((NZ, 2, PART, W), BF16),
            pltpu.VMEM((NZ, 2, PART, W), BF16),
            pltpu.SemaphoreType.DMA((9,)),
            pltpu.SemaphoreType.DMA((N_COPIES,)),
            pltpu.SemaphoreType.DMA((N_COPIES,)),
        ],
        compiler_params=pltpu.CompilerParams(
            collective_id=0, has_side_effects=True, vmem_limit_bytes=60 * 1024 * 1024
        ),
    )(
        points,
        anchor_index.reshape(1, -1),
        tile_branch,
        norm_gain.reshape(1, -1),
        q_surface,
        q_volume,
        kv_weight,
        out_weight,
    )
    return both[0], both[1]


def solution(mesh):
    in_specs = (
        P(("pt", "anc"), "head"),
        P(),
        P(("pt", "anc")),
        P(),
        P(None, "head"),
        P(None, "head"),
        P(None, None, "head"),
        P("head", None),
    )
    out_specs = (P(("pt", "anc"), "head"), P(("pt", "anc"), "head"))
    return jax.shard_map(shards, mesh=mesh, in_specs=in_specs, out_specs=out_specs, check_vma=False)
```
